512 devices in a mesh: group: 16 (over z_lo, y), vocab: 32 (over x, z_hi, core).
Axes of the slice: x: 4, y: 4, z: 16 (z_hi: 4, z_lo: 4; z = z_hi * 4 + z_lo), core: 2. Of those that a mesh axis runs over, the one named last changes fastest.
Arguments:
- teacher_rows: bfloat16 [4096, 4096], P(('group', 'vocab')), may hold values from -8 to 8
- student_rows: bfloat16 [4096, 5120], P(('group', 'vocab')), may hold values from -8 to 8
- teacher_gain: bfloat16 [4096], replicated, may hold values from 0.25 to 1.75
- student_gain: bfloat16 [5120], replicated, may hold values from 0.25 to 1.75
- teacher_head: bfloat16 [4096, 8192], P(None, 'vocab'), may hold values from -8 to 8
- student_head: bfloat16 [5120, 8192], P(None, 'vocab'), may hold values from -8 to 8
- route: int32 [4096], replicated, may hold values from 0 to 15, as said below
- target: int32 [4096], P('group'), may hold values from 0 to 8191
Outputs:
- token_loss: float32 [4096], P('group')
- row_grad: bfloat16 [4096, 5120], P(('group', 'vocab'))
The draws below stay inside these ranges and needn't reach their ends.
Inputs may be any that keep to these rules, and one draw needn't show every extreme that they name: route[r] is the student group of teacher row r. For every v, each student group receives exactly 8 of the rows r with (r % 256) // 8 = v, and the 8 rows t * 256 + v * 8 + k of one t and v send to each student group either none or exactly 1 row.
All inputs are finite; a program needn't handle non-finite values.
Results may differ from the reference program's by a relative error of at most 0.019.
Values may be sent and summed in bfloat16 or wider, within the bound.
A program may use at most 64 MiB of HBM per device.

```python
import math
import jax
import jax.numpy as jnp
from jax import lax

DT = 4096
DS = 5120
VD = 256
ROWS = 256
RD = 8
TOKENS = 4096
VOCAB = 8192
N_GROUP = 16
N_VOCAB = 32


def spike_plan(key, row_total, column_total, width, salt):
    key = jax.random.fold_in(key, salt)
    sub_keys = jax.random.split(key, 4)
    picked_rows = jax.random.permutation(sub_keys[0], row_total)[:8]
    picked_columns = jax.random.permutation(sub_keys[1], column_total)[:16]
    sign_rows = (2 * jax.random.randint(sub_keys[2], (8, width), 0, 2) - 1).astype(jnp.float32)
    levels = 140.0 + 14.0 * jnp.arange(8, dtype=jnp.float32)[:, None]
    strength = (levels + jax.random.uniform(sub_keys[3], (8, 1), jnp.float32, 0.0, 4.0)) / width
    return (picked_rows, picked_columns, sign_rows, strength)


def row_values(noise, scale_key, row_total):
    row_scale = jnp.exp(jax.random.uniform(scale_key, (row_total, 1), jnp.float32, math.log(0.5), math.log(2.0)))
    return jnp.clip(noise * row_scale, -8.0, 8.0)


def head_values(noise, scale_key, width, column_total):
    column_scale = jnp.exp(jax.random.uniform(scale_key, (1, column_total), jnp.float32, math.log(1.5), math.log(6.0)))
    return noise * column_scale / math.sqrt(width)


def draw_teacher_rows(key, part):
    plan = spike_plan(key, TOKENS, VOCAB, DT, 21)
    key = jax.random.fold_in(key, 1)
    sub_keys = jax.random.split(key, 2)
    noise = jax.random.truncated_normal(sub_keys[0], -4.0, 4.0, (TOKENS, DT), jnp.float32)
    values = row_values(noise, sub_keys[1], TOKENS)
    return values.at[plan[0]].set(1.5 * plan[2]).astype(jnp.bfloat16)


def draw_student_rows(key, part):
    plan = spike_plan(key, TOKENS, VOCAB, DS, 22)
    key = jax.random.fold_in(key, 2)
    sub_keys = jax.random.split(key, 2)
    noise = jax.random.truncated_normal(sub_keys[0], -4.0, 4.0, (TOKENS, DS), jnp.float32)
    values = row_values(noise, sub_keys[1], TOKENS)
    return values.at[plan[0]].set(1.5 * plan[2]).astype(jnp.bfloat16)


def draw_teacher_head(key, part):
    plan = spike_plan(key, TOKENS, VOCAB, DT, 21)
    key = jax.random.fold_in(key, 3)
    sub_keys = jax.random.split(key, 2)
    noise = jax.random.truncated_normal(sub_keys[0], -4.0, 4.0, (DT, VOCAB), jnp.float32)
    values = head_values(noise, sub_keys[1], DT, VOCAB)
    aligned = jnp.transpose(plan[2] * plan[3])
    values = values.at[:, plan[1][:8]].set(aligned)
    values = values.at[:, plan[1][8:]].set(0.992 * aligned)
    return jnp.clip(values, -8.0, 8.0).astype(jnp.bfloat16)


def draw_student_head(key, part):
    plan = spike_plan(key, TOKENS, VOCAB, DS, 22)
    key = jax.random.fold_in(key, 4)
    sub_keys = jax.random.split(key, 2)
    noise = jax.random.truncated_normal(sub_keys[0], -4.0, 4.0, (DS, VOCAB), jnp.float32)
    values = head_values(noise, sub_keys[1], DS, VOCAB)
    aligned = jnp.transpose(plan[2] * plan[3])
    values = values.at[:, plan[1][:8]].set(aligned)
    values = values.at[:, plan[1][8:]].set(0.992 * aligned)
    return jnp.clip(values, -8.0, 8.0).astype(jnp.bfloat16)


def draw_route(key, part):
    key = jax.random.fold_in(key, 5)
    share = min(N_GROUP, RD)

    def one_index(vocab_key):
        sub_keys = jax.random.split(vocab_key, 3)
        shifts = jax.random.permutation(sub_keys[0], N_GROUP)
        labels = jax.random.permutation(sub_keys[1], N_GROUP)
        offsets = jax.random.permutation(sub_keys[2], RD) % share
        return labels[(shifts[:, None] + offsets[None, :]) % N_GROUP]
    blocks = jax.vmap(one_index)(jax.random.split(key, N_VOCAB))
    return jnp.transpose(blocks, (1, 0, 2)).reshape(TOKENS).astype(jnp.int32)


def plant(array, stream_key, least, top_value):
    shape = array.shape
    spot = [jax.random.randint(jax.random.fold_in(stream_key, axis), (), 0, shape[axis]) for axis in range(len(shape))]
    array = array.at[tuple(spot)].set(least)
    longest = shape.index(max(shape))
    spot[longest] = (spot[longest] + 1) % shape[longest]
    return array.at[tuple(spot)].set(top_value)


def setup_inputs(seed: int = 0) -> dict:
    key_of = jax.random.split(jax.random.key(seed), 9)
    return {
        "teacher_rows": draw_teacher_rows(jax.random.fold_in(key_of[8], 71), 0),
        "student_rows": draw_student_rows(jax.random.fold_in(key_of[8], 71), 0),
        "teacher_gain": jnp.clip(1.0 + 0.15 * jax.random.normal(key_of[2], (DT,), jnp.float32), 0.25, 1.75).astype(jnp.bfloat16),
        "student_gain": jnp.clip(1.0 + 0.15 * jax.random.normal(key_of[3], (DS,), jnp.float32), 0.25, 1.75).astype(jnp.bfloat16),
        "teacher_head": draw_teacher_head(jax.random.fold_in(key_of[8], 71), 0),
        "student_head": draw_student_head(jax.random.fold_in(key_of[8], 71), 0),
        "route": draw_route(jax.random.fold_in(key_of[8], 71), 0),
        "target": plant(jax.random.randint(key_of[7], (TOKENS,), 0, VOCAB), jax.random.fold_in(key_of[7], 1), 0, VOCAB - 1).astype(jnp.int32),
    }


epsilon = 1e-06
loss_scale = 16.0
distill_mix = 0.5

def normalize_rows(rows):
    widened = rows.astype(jnp.float32)
    inverse = lax.rsqrt(lax.optimization_barrier(jnp.mean(widened * widened, axis=1, keepdims=True)) + epsilon)
    return (widened * inverse, inverse)

def student_places(route):
    blocks = route.reshape(N_GROUP, N_VOCAB, RD).transpose(1, 0, 2).reshape(N_VOCAB, N_GROUP * RD)
    positions = jnp.arange(N_GROUP * RD, dtype=jnp.int32)
    earlier = positions[:, None] < positions[None, :]

    def rank_block(destinations):
        same_route = destinations[:, None] == destinations[None, :]
        return lax.optimization_barrier(jnp.sum(jnp.where(same_route & earlier, 1, 0), axis=0)).astype(jnp.int32)
    rank_table = lax.map(rank_block, blocks)
    rank_table = rank_table.reshape(N_VOCAB, N_GROUP, RD).transpose(1, 0, 2).reshape(TOKENS)
    vocab_index = jnp.arange(TOKENS, dtype=jnp.int32) % ROWS // RD
    return (route * ROWS + vocab_index * RD + rank_table).astype(jnp.int32)

def reference(teacher_rows, student_rows, teacher_gain, student_gain, teacher_head, student_head, route, target):
    teacher_hat = normalize_rows(teacher_rows)[0]
    teacher_normed = (teacher_hat * teacher_gain.astype(jnp.float32)).astype(jnp.bfloat16)
    routed = jnp.zeros((TOKENS, DT), teacher_normed.dtype).at[student_places(route)].set(teacher_normed)
    student_hat, inverse = normalize_rows(student_rows)
    gain_wide = student_gain.astype(jnp.float32)
    student_normed = (student_hat * gain_wide).astype(jnp.bfloat16)
    vocab_ids = jnp.arange(VOCAB, dtype=jnp.int32)

    def group_terms(pieces):
        group_routed, group_student, group_target, group_hat, group_inverse = pieces
        teacher_logits = jnp.dot(group_routed, teacher_head, preferred_element_type=jnp.float32)
        student_logits = jnp.dot(group_student, student_head, preferred_element_type=jnp.float32)
        teacher_top = lax.optimization_barrier(jnp.max(teacher_logits, axis=1, keepdims=True))
        student_top = lax.optimization_barrier(jnp.max(student_logits, axis=1, keepdims=True))
        teacher_exp = jnp.exp(teacher_logits - teacher_top)
        student_exp = jnp.exp(student_logits - student_top)
        teacher_sum = lax.optimization_barrier(jnp.sum(teacher_exp, axis=1))
        student_sum = lax.optimization_barrier(jnp.sum(student_exp, axis=1))
        cross_sum = lax.optimization_barrier(jnp.sum(teacher_exp * (teacher_logits - student_logits), axis=1))
        is_target = vocab_ids[None, :] == group_target[:, None]
        picked = lax.optimization_barrier(jnp.sum(jnp.where(is_target, student_logits, 0.0), axis=1))
        teacher_lse = teacher_top[:, 0] + jnp.log(teacher_sum)
        student_lse = student_top[:, 0] + jnp.log(student_sum)
        token_loss = distill_mix * (cross_sum / teacher_sum - teacher_lse + student_lse) + (1.0 - distill_mix) * (student_lse - picked)
        logit_grad = (loss_scale * (student_exp / student_sum[:, None] - distill_mix * teacher_exp / teacher_sum[:, None] - (1.0 - distill_mix) * jnp.where(is_target, 1.0, 0.0))).astype(jnp.bfloat16)

        def add_block(running, shard_index):
            grad_block = lax.dynamic_slice_in_dim(logit_grad, shard_index * VD, VD, 1)
            head_block = lax.dynamic_slice_in_dim(student_head, shard_index * VD, VD, 1)
            partial_sum = lax.dot_general(grad_block, head_block, (((1,), (1,)), ((), ())), preferred_element_type=jnp.float32)
            rounded = lax.optimization_barrier(partial_sum.astype(jnp.bfloat16))
            return (running + rounded.astype(jnp.float32), None)
        head_grad = lax.scan(add_block, jnp.zeros((ROWS, DS), jnp.float32), jnp.arange(N_VOCAB, dtype=jnp.int32))[0]
        scaled_grad = head_grad * gain_wide
        row_grad = group_inverse * (scaled_grad - group_hat * lax.optimization_barrier(jnp.mean(scaled_grad * group_hat, axis=1, keepdims=True)))
        return (token_loss, row_grad.astype(jnp.bfloat16))
    pieces = (routed.reshape(N_GROUP, ROWS, DT), student_normed.reshape(N_GROUP, ROWS, DS), target.reshape(N_GROUP, ROWS), student_hat.reshape(N_GROUP, ROWS, DS), inverse.reshape(N_GROUP, ROWS, 1))
    token_loss, row_grad = lax.map(group_terms, pieces)
    return (token_loss.reshape(TOKENS), row_grad.reshape(TOKENS, DS))
```

```python
import functools

import jax
import jax.numpy as jnp
from jax import lax
from jax.experimental import pallas as pl
from jax.experimental.pallas import tpu as pltpu
from jax.sharding import PartitionSpec as P

MESH = pl.DeviceIdType.MESH
epsilon = 1e-06
loss_scale = 16.0
distill_mix = 0.5

RING = 4
CORES = 2
SUB = 16


def contract_last(left_side, right_side):
    return lax.dot_general(
        left_side, right_side, (((1,), (1,)), ((), ())), preferred_element_type=jnp.float32
    )


class Gather:
    def __init__(self, buf, send, recv, place):
        self.buf, self.send, self.recv, self.place = buf, send, recv, place
        self.started = []
        self.core_left = []

    def copy(self, index, cols, xx, zz, dev):
        view = self.buf.at[cols, self.place.rows(xx, zz), :]
        return pltpu.make_async_remote_copy(
            src_ref=view,
            dst_ref=view,
            send_sem=self.send.at[index],
            recv_sem=self.recv.at[index],
            device_id=dev,
            device_id_type=MESH,
        )

    def go(self, *args):
        copy = self.copy(*args)
        copy.start()
        self.started.append(copy)
        return copy

    def half(self):
        return pl.ds(self.place.core * 2, 2)

    def quarter(self, h):
        return pl.ds(self.place.core * 2 + h, 1)

    def z_near(self):
        p = self.place
        self.zp = self.go(0, self.half(), p.x, p.zh, p.dev(p.x, p.zh + 1, p.core))
        self.zm = self.go(1, self.half(), p.x, p.zh, p.dev(p.x, p.zh - 1, p.core))
        self.x_near(0)

    def x_near(self, j):
        p = self.place
        zz = p.zh + (0, -1, 1, 2)[j]
        self.go(4 + 4 * j, self.half(), p.x, zz, p.dev(p.x + 1, p.zh, p.core))
        self.go(5 + 4 * j, self.half(), p.x, zz, p.dev(p.x - 1, p.zh, p.core))

    def to_core(self, index, xx, zz):
        p = self.place
        self.core_left.append(self.go(index, self.half(), xx, zz, p.dev(p.x, p.zh, 1 - p.core)))

    def z_from_minus(self):
        p = self.place
        self.zp.wait_recv()
        self.zfp = self.go(2, self.quarter(0), p.x, p.zh - 1, p.dev(p.x, p.zh + 1, p.core))
        self.x_near(1)
        self.to_core(20, p.x, p.zh - 1)

    def z_from_plus(self):
        p = self.place
        self.zm.wait_recv()
        self.zfm = self.go(3, self.quarter(1), p.x, p.zh + 1, p.dev(p.x, p.zh - 1, p.core))
        self.x_near(2)
        self.to_core(21, p.x, p.zh + 1)

    def z_far(self):
        p = self.place
        self.zfp.wait_recv()
        self.zfm.wait_recv()
        self.x_near(3)
        self.to_core(22, p.x, p.zh + 2)

    def x_from_near(self, j):
        p = self.place
        zz = p.zh + (0, -1, 1, 2)[j]
        plus, minus = p.dev(p.x + 1, p.zh, p.core), p.dev(p.x - 1, p.zh, p.core)
        self.copy(4 + 4 * j, self.half(), p.x - 1, zz, plus).wait_recv()
        self.go(6 + 4 * j, self.quarter(0), p.x - 1, zz, plus)
        self.to_core(23 + 3 * j, p.x - 1, zz)
        self.copy(5 + 4 * j, self.half(), p.x + 1, zz, minus).wait_recv()
        self.go(7 + 4 * j, self.quarter(1), p.x + 1, zz, minus)
        self.to_core(24 + 3 * j, p.x + 1, zz)

    def x_far(self, j):
        p = self.place
        zz = p.zh + (0, -1, 1, 2)[j]
        plus, minus = p.dev(p.x + 1, p.zh, p.core), p.dev(p.x - 1, p.zh, p.core)
        self.copy(6 + 4 * j, self.quarter(0), p.x + 2, zz, plus).wait_recv()
        self.copy(7 + 4 * j, self.quarter(1), p.x + 2, zz, minus).wait_recv()
        self.to_core(25 + 3 * j, p.x + 2, zz)

    def from_core(self):
        for copy in self.core_left:
            copy.wait_recv()


GATHER_COPIES = 35


class Place:
    def __init__(self):
        self.group = lax.axis_index("group")
        self.vocab = lax.axis_index("vocab")
        self.core = lax.rem(self.vocab, CORES)
        self.zh = lax.rem(self.vocab // CORES, RING)
        self.x = self.vocab // (CORES * RING)

    def dev(self, xx, zz, cc):
        xx, zz = lax.rem(xx + RING, RING), lax.rem(zz + RING, RING)
        return (self.group, (xx * RING + zz) * CORES + cc)

    def rows(self, xx, zz):
        xx, zz = lax.rem(xx + RING, RING), lax.rem(zz + RING, RING)
        return pl.ds(pl.multiple_of((xx * RING + zz) * 16, 16), 16)


def kernel(
    groups,
    teacher_rows,
    student_rows,
    teacher_gain,
    student_gain,
    teacher_head,
    student_head,
    route,
    target,
    loss_out,
    grad_out,
    head_t,
    head_s,
    rows_t,
    rows_s,
    wide,
    out_rows,
    in_rows,
    pair_t_out,
    pair_t_in,
    pair_s_out,
    pair_s_in,
    inverse_keep,
    exp_t,
    exp_s,
    keep_s,
    logit_grad,
    stat_one,
    stat_two,
    own_part,
    pair_out,
    pair_in,
    xf_out,
    xf_in,
    xn_out,
    xn_in,
    z_part,
    zf_out,
    zf_in,
    zn_out,
    zn_in,
    mine,
    last_out,
    last_in,
    local_sem,
    pair_sem,
    route_sem,
    gather_t_sem,
    gather_s_sem,
    stat_sem,
    back_sem,
):
    p = Place()
    g, v, core, zh, x = p.group, p.vocab, p.core, p.zh, p.x
    local_rows = teacher_rows.shape[0]
    dt, ds = teacher_rows.shape[1], student_rows.shape[1]
    wt, ws = dt // 4, ds // 4
    chunk = dt // SUB
    other = p.dev(x, zh, 1 - core)
    f32, bf16 = jnp.float32, jnp.bfloat16
    sends = []

    def remote(src, dst, sem, index, dev):
        copy = pltpu.make_async_remote_copy(
            src_ref=src,
            dst_ref=dst,
            send_sem=sem.at[0, index],
            recv_sem=sem.at[1, index],
            device_id=dev,
            device_id_type=MESH,
        )
        copy.start()
        sends.append(copy)
        return copy

    barrier = pltpu.get_barrier_semaphore()
    flat = x * CORES + core

    def near(d):
        f = lax.rem(flat + d, RING * CORES)
        return f

    def near_dev(d):
        f = near(d)
        return p.dev(f // CORES, zh, lax.rem(f, CORES))

    for d in range(1, groups):
        pl.semaphore_signal(
            barrier, inc=1, device_id=(lax.rem(g + d, groups), v), device_id_type=MESH
        )
    for d in range(1, RING):
        pl.semaphore_signal(
            barrier, inc=1, device_id=p.dev(x, zh + d, core), device_id_type=MESH
        )
    for d in range(1, RING * CORES):
        pl.semaphore_signal(barrier, inc=1, device_id=near_dev(d), device_id_type=MESH)

    load_s = pltpu.make_async_copy(student_head, head_s, local_sem.at[0])
    load_t = pltpu.make_async_copy(teacher_head, head_t, local_sem.at[1])
    load_s.start()
    load_t.start()

    wide_s = student_rows[...].astype(f32)
    inverse = lax.rsqrt(jnp.mean(wide_s * wide_s, axis=1, keepdims=True) + epsilon)
    inverse_keep[...] = jnp.broadcast_to(inverse, inverse_keep.shape)
    pair_s_out[...] = (
        (wide_s * inverse * student_gain[...].astype(f32)).astype(bf16).astype(f32)
    )
    wide_t = teacher_rows[...].astype(f32)
    inverse_t = lax.rsqrt(jnp.mean(wide_t * wide_t, axis=1, keepdims=True) + epsilon)
    normed_t = (wide_t * inverse_t * teacher_gain[...].astype(f32)).astype(bf16).astype(f32)
    for c in range(SUB):
        wide[:, c, :] = normed_t[:, c * chunk : (c + 1) * chunk]
    first = (g * lax.axis_size("vocab") + v) * local_rows
    my_routes = [route[first + k] for k in range(local_rows)]

    @pl.loop(0, groups)
    def _(dest):
        total = jnp.zeros((SUB, chunk), f32)
        for k in range(local_rows):
            total += jnp.where(my_routes[k] == dest, 1.0, 0.0) * wide[k]
        out_rows[dest] = total.astype(bf16)

    in_rows[g] = out_rows[g]

    pl.semaphore_wait(barrier, groups - 1 + RING - 1 + RING * CORES - 1)

    pair_s = remote(pair_s_out, pair_s_in, pair_sem, 0, other)
    routed_copies = []
    for d in range(1, groups):
        dest = lax.rem(g + d, groups)
        routed_copies.append(
            remote(out_rows.at[dest], in_rows.at[g], route_sem, d, (dest, v))
        )

    def own_block(rows, pair_out_ref, pair_in_ref, width):
        mine_rows, their_rows = pair_out_ref[...], pair_in_ref[...]
        is_first = core == 0
        both = jnp.concatenate(
            [
                jnp.where(is_first, mine_rows, their_rows),
                jnp.where(is_first, their_rows, mine_rows),
            ],
            axis=0,
        ).astype(bf16)
        for q in range(4):
            rows[q, p.rows(x, zh), :] = both[:, q * width : (q + 1) * width]

    student = Gather(rows_s, gather_s_sem.at[0], gather_s_sem.at[1], p)
    teacher = Gather(rows_t, gather_t_sem.at[0], gather_t_sem.at[1], p)

    pair_s.wait_recv()
    own_block(rows_s, pair_s_out, pair_s_in, ws)
    student.z_near()

    ranks, valids = [], []
    seen = jnp.int32(0)
    for t in range(groups):
        start = (t * lax.axis_size("vocab") + v) * local_rows
        valid = jnp.int32(0)
        for k in range(local_rows):
            valid += jnp.where(route[start + k] == g, 1, 0)
        ranks.append(seen)
        valids.append(valid)
        seen = seen + valid
    for copy in routed_copies:
        copy.wait_recv()
    for j in range(local_rows):
        total = jnp.zeros((SUB, chunk), f32)
        for t in range(groups):
            weight = jnp.where(ranks[t] == j, valids[t], 0).astype(f32)
            total += weight * in_rows[t].astype(f32)
        wide[j] = total
    for c in range(SUB):
        pair_t_out[:, c * chunk : (c + 1) * chunk] = wide[:, c, :]
    pair_t = remote(pair_t_out, pair_t_in, pair_sem, 1, other)
    pair_t.wait_recv()
    own_block(rows_t, pair_t_out, pair_t_in, wt)
    teacher.z_near()

    student.z_from_minus()
    student.z_from_plus()
    student.x_from_near(0)
    student.x_far(0)
    student.z_far()
    student.x_from_near(1)
    student.x_from_near(2)
    teacher.z_from_minus()
    teacher.z_from_plus()
    student.x_far(1)
    student.x_far(2)
    student.x_from_near(3)
    teacher.x_from_near(0)
    teacher.x_far(0)
    student.x_far(3)
    student.from_core()
    teacher.z_far()
    teacher.x_from_near(1)
    teacher.x_from_near(2)

    load_s.wait()
    total = jnp.zeros((logit_grad.shape[0], head_s.shape[1]), f32)
    for q in range(4):
        total += jnp.dot(
            rows_s[q], head_s[q * ws : (q + 1) * ws, :], preferred_element_type=f32
        )
    logits_s = jnp.transpose(total)
    top_s = jnp.max(logits_s, axis=0, keepdims=True)
    keep_s[...] = logits_s
    powers = jnp.exp(logits_s - top_s)
    exp_s[...] = powers
    sum_s = jnp.sum(powers, axis=0, keepdims=True)
    shard = head_s.shape[1]
    columns = v * shard + lax.broadcasted_iota(jnp.int32, exp_s.shape, 0)
    picked = jnp.sum(
        jnp.where(columns == target[...], logits_s, 0.0), axis=0, keepdims=True
    )

    teacher.x_far(1)
    teacher.x_far(2)
    teacher.x_from_near(3)
    teacher.x_far(3)
    teacher.from_core()

    load_t.wait()
    total = jnp.zeros((logit_grad.shape[0], head_t.shape[1]), f32)
    for q in range(4):
        total += jnp.dot(
            rows_t[q], head_t[q * wt : (q + 1) * wt, :], preferred_element_type=f32
        )
    logits_t = jnp.transpose(total)
    top_t = jnp.max(logits_t, axis=0, keepdims=True)
    powers = jnp.exp(logits_t - top_t)
    exp_t[...] = powers
    sum_t = jnp.sum(powers, axis=0, keepdims=True)
    cross = jnp.sum(powers * (logits_t - keep_s[...]), axis=0, keepdims=True)

    stats = jnp.concatenate(
        [top_t, top_s, top_t, jnp.zeros_like(top_t), sum_t, sum_s, cross, picked], axis=0
    )

    def merge(slots, count):
        parts = [slots[i] for i in range(count)]
        top = functools.reduce(jnp.maximum, [part[0:4] for part in parts])
        sums = sum(jnp.exp(part[0:4] - top) * part[4:8] for part in parts)
        return jnp.concatenate([top, sums], axis=0)

    stat_one[flat] = stats
    copies = [
        remote(stat_one.at[flat], stat_one.at[flat], stat_sem, d, near_dev(d))
        for d in range(1, RING * CORES)
    ]
    for copy in copies:
        copy.wait_recv()
    stat_two[zh] = merge(stat_one, RING * CORES)
    copies = [
        remote(
            stat_two.at[zh],
            stat_two.at[zh],
            stat_sem,
            RING * CORES + d,
            p.dev(x, zh + d, core),
        )
        for d in range(1, RING)
    ]
    for copy in copies:
        copy.wait_recv()
    merged = merge(stat_two, RING)
    all_top_t, all_top_s = merged[0:1], merged[1:2]
    all_sum_t, all_sum_s = merged[4:5], merged[5:6]
    scale_s = loss_scale * jnp.exp(top_s - all_top_s) / all_sum_s
    scale_t = (loss_scale * distill_mix) * jnp.exp(top_t - all_top_t) / all_sum_t
    gradient = (
        exp_s[...] * scale_s
        - exp_t[...] * scale_t
        - jnp.where(columns == target[...], loss_scale * (1.0 - distill_mix), 0.0)
    )
    logit_grad[...] = jnp.transpose(gradient).astype(bf16)

    order = (2, 1, -1, 0)
    plus_x, minus_x = p.dev(x + 1, zh, core), p.dev(x - 1, zh, core)
    plus_z, minus_z = p.dev(x, zh + 1, core), p.dev(x, zh - 1, core)
    pair_copies, far_copies, near_copies = {}, {}, {}

    def head_quarter(q):
        return head_s[pl.ds(pl.multiple_of(q * ws, ws), ws), :]

    def multiply(i):
        zz = zh + order[i]
        left = jnp.concatenate(
            [logit_grad[p.rows(x + d, zz), :] for d in order], axis=0
        )
        for h in range(2):
            pair_out[i, h] = contract_last(
                left, head_quarter((1 - core) * 2 + h)
            ).astype(bf16)
        pair_copies[i] = remote(pair_out.at[i], pair_in.at[i], back_sem, i, other)
        for h in range(2):
            own_part[i, h] = contract_last(left, head_quarter(core * 2 + h))

    def x_far(i):
        pair_copies[i].wait_recv()
        own_part[i] = own_part[i] + pair_in[i].astype(f32)
        xf_out[i] = own_part[i, :, 0:16, :].astype(bf16)
        far_copies[i] = (
            remote(xf_out.at[i, 0], xf_in.at[i, 0], back_sem, 4 + 2 * i, plus_x),
            remote(xf_out.at[i, 1], xf_in.at[i, 1], back_sem, 5 + 2 * i, minus_x),
        )

    def x_near(i):
        far_copies[i][0].wait_recv()
        xn_out[i, 0, 0] = (own_part[i, 0, 16:32, :] + xf_in[i, 0].astype(f32)).astype(bf16)
        xn_out[i, 0, 1] = own_part[i, 1, 16:32, :].astype(bf16)
        up = remote(xn_out.at[i, 0], xn_in.at[i, 0], back_sem, 12 + 2 * i, plus_x)
        far_copies[i][1].wait_recv()
        xn_out[i, 1, 0] = own_part[i, 0, 32:48, :].astype(bf16)
        xn_out[i, 1, 1] = (own_part[i, 1, 32:48, :] + xf_in[i, 1].astype(f32)).astype(bf16)
        down = remote(xn_out.at[i, 1], xn_in.at[i, 1], back_sem, 13 + 2 * i, minus_x)
        near_copies[i] = (up, down)

    def x_done(i):
        for copy in near_copies[i]:
            copy.wait_recv()
        return (
            own_part[i, :, 48:64, :] + xn_in[i, 0].astype(f32) + xn_in[i, 1].astype(f32)
        )

    multiply(0)
    multiply(1)
    x_far(0)
    multiply(2)
    x_far(1)
    x_near(0)
    multiply(3)
    x_far(2)
    x_near(1)
    zf_out[...] = x_done(0).astype(bf16)
    z_far = (
        remote(zf_out.at[0], zf_in.at[0], back_sem, 20, plus_z),
        remote(zf_out.at[1], zf_in.at[1], back_sem, 21, minus_z),
    )
    x_far(3)
    x_near(2)
    z_part[0] = x_done(1)
    z_far[0].wait_recv()
    zn_out[0, 0] = (z_part[0, 0] + zf_in[0].astype(f32)).astype(bf16)
    zn_out[0, 1] = z_part[0, 1].astype(bf16)
    z_up = remote(zn_out.at[0], zn_in.at[0], back_sem, 22, plus_z)
    x_near(3)
    z_part[1] = x_done(2)
    z_far[1].wait_recv()
    zn_out[1, 0] = z_part[1, 0].astype(bf16)
    zn_out[1, 1] = (z_part[1, 1] + zf_in[1].astype(f32)).astype(bf16)
    z_down = remote(zn_out.at[1], zn_in.at[1], back_sem, 23, minus_z)
    z_part[2] = x_done(3)

    lse_t = all_top_t + jnp.log(all_sum_t)
    lse_s = all_top_s + jnp.log(all_sum_s)
    loss_out[...] = distill_mix * (merged[6:7] / all_sum_t - lse_t + lse_s) + (
        1.0 - distill_mix
    ) * (lse_s - merged[7:8])
    inverse = inverse_keep[:, 0:1]
    hat = student_rows[...].astype(f32) * inverse
    gain = student_gain[...].astype(f32)

    z_up.wait_recv()
    z_down.wait_recv()
    mine[...] = z_part[2] + zn_in[0].astype(f32) + zn_in[1].astype(f32)
    last_out[...] = mine[:, pl.ds(pl.multiple_of((1 - core) * 8, 8), 8), :]
    last = remote(last_out, last_in, back_sem, 24, other)
    kept = mine[:, pl.ds(pl.multiple_of(core * 8, 8), 8), :]
    last.wait_recv()
    theirs = last_in[...]
    is_first = core == 0
    head_grad = jnp.concatenate(
        [
            jnp.where(is_first, kept[0], theirs[0]),
            jnp.where(is_first, kept[1], theirs[1]),
            jnp.where(is_first, theirs[0], kept[0]),
            jnp.where(is_first, theirs[1], kept[1]),
        ],
        axis=1,
    )
    scaled = head_grad * gain
    grad_out[...] = (
        inverse * (scaled - hat * jnp.mean(scaled * hat, axis=1, keepdims=True))
    ).astype(bf16)

    for copy in sends + student.started + teacher.started:
        copy.wait_send()


def local(
    teacher_rows,
    student_rows,
    teacher_gain,
    student_gain,
    teacher_head,
    student_head,
    route,
    target,
):
    groups = lax.axis_size("group")
    f32, bf16 = jnp.float32, jnp.bfloat16
    local_rows, dt = teacher_rows.shape
    ds = student_rows.shape[1]
    shard = teacher_head.shape[1]
    rows = target.shape[0]
    wt, ws, chunk = dt // 4, ds // 4, dt // SUB
    vmem = pl.BlockSpec(memory_space=pltpu.VMEM)
    hbm = pl.BlockSpec(memory_space=pl.ANY)
    loss, grad = pl.pallas_call(
        functools.partial(kernel, groups),
        out_shape=(
            jax.ShapeDtypeStruct((1, rows), f32),
            jax.ShapeDtypeStruct((local_rows, ds), bf16),
        ),
        in_specs=[
            vmem,
            vmem,
            vmem,
            vmem,
            hbm,
            hbm,
            pl.BlockSpec(memory_space=pltpu.SMEM),
            vmem,
        ],
        out_specs=(vmem, vmem),
        scratch_shapes=[
            pltpu.VMEM((dt, shard), bf16),
            pltpu.VMEM((ds, shard), bf16),
            pltpu.VMEM((4, rows, wt), bf16),
            pltpu.VMEM((4, rows, ws), bf16),
            pltpu.VMEM((local_rows, SUB, chunk), f32),
            pltpu.VMEM((groups, SUB, chunk), bf16),
            pltpu.VMEM((groups, SUB, chunk), bf16),
            pltpu.VMEM((local_rows, dt), f32),
            pltpu.VMEM((local_rows, dt), f32),
            pltpu.VMEM((local_rows, ds), f32),
            pltpu.VMEM((local_rows, ds), f32),
            pltpu.VMEM((local_rows, 128), f32),
            pltpu.VMEM((shard, rows), f32),
            pltpu.VMEM((shard, rows), f32),
            pltpu.VMEM((shard, rows), f32),
            pltpu.VMEM((rows, shard), bf16),
            pltpu.VMEM((RING * CORES, 8, rows), f32),
            pltpu.VMEM((RING, 8, rows), f32),
            pltpu.VMEM((4, 2, 64, ws), f32),
            pltpu.VMEM((4, 2, 64, ws), bf16),
            pltpu.VMEM((4, 2, 64, ws), bf16),
            pltpu.VMEM((4, 2, 16, ws), bf16),
            pltpu.VMEM((4, 2, 16, ws), bf16),
            pltpu.VMEM((4, 2, 2, 16, ws), bf16),
            pltpu.VMEM((4, 2, 2, 16, ws), bf16),
            pltpu.VMEM((3, 2, 16, ws), f32),
            pltpu.VMEM((2, 16, ws), bf16),
            pltpu.VMEM((2, 16, ws), bf16),
            pltpu.VMEM((2, 2, 16, ws), bf16),
            pltpu.VMEM((2, 2, 16, ws), bf16),
            pltpu.VMEM((2, 16, ws), f32),
            pltpu.VMEM((2, 8, ws), f32),
            pltpu.VMEM((2, 8, ws), f32),
            pltpu.SemaphoreType.DMA((2,)),
            pltpu.SemaphoreType.DMA((2, 2)),
            pltpu.SemaphoreType.DMA((2, groups)),
            pltpu.SemaphoreType.DMA((2, GATHER_COPIES)),
            pltpu.SemaphoreType.DMA((2, GATHER_COPIES)),
            pltpu.SemaphoreType.DMA((2, RING * CORES + RING)),
            pltpu.SemaphoreType.DMA((2, 25)),
        ],
        compiler_params=pltpu.CompilerParams(
            collective_id=0, has_side_effects=True, vmem_limit_bytes=48 * 1024 * 1024
        ),
        name="distill",
    )(
        teacher_rows,
        student_rows,
        teacher_gain.reshape(1, dt),
        student_gain.reshape(1, ds),
        teacher_head,
        student_head,
        route,
        target.reshape(1, rows),
    )
    return (loss.reshape(rows), grad)


def solution(mesh):
    placed = (
        P(("group", "vocab"), None),
        P(("group", "vocab"), None),
        P(),
        P(),
        P(None, "vocab"),
        P(None, "vocab"),
        P(),
        P("group"),
    )
    return jax.shard_map(
        local,
        mesh=mesh,
        in_specs=placed,
        out_specs=(P("group"), P(("group", "vocab"), None)),
        check_vma=False,
    )
```

```python
import functools

import jax
import jax.numpy as jnp
from jax import lax
from jax.experimental import pallas as pl
from jax.experimental.pallas import tpu as pltpu
from jax.sharding import PartitionSpec as P

MESH = pl.DeviceIdType.MESH
epsilon = 1e-06
loss_scale = 16.0
distill_mix = 0.5

RING = 4
CORES = 2
BLOCKS = RING * RING
SUB = 16
STEPS = (0, -1, 1, 2)
GATHER_COPIES = 6 + 6 * RING


def contract_last(left_side, right_side):
    return lax.dot_general(
        left_side, right_side, (((1,), (1,)), ((), ())), preferred_element_type=jnp.float32
    )


class Place:
    def __init__(self):
        self.group = lax.axis_index("group")
        self.vocab = lax.axis_index("vocab")
        self.core = lax.rem(self.vocab, CORES)
        self.zh = lax.rem(self.vocab // CORES, RING)
        self.x = self.vocab // (CORES * RING)

    def block(self, dx, dz):
        xx, zz = lax.rem(self.x + dx + RING, RING), lax.rem(self.zh + dz + RING, RING)
        return xx * RING + zz

    def dev(self, dx, dz):
        return (self.group, self.block(dx, dz) * CORES + self.core)

    def nth(self, d):
        return (self.group, lax.rem(self.block(0, 0) + d, BLOCKS) * CORES + self.core)

    def other(self):
        return (self.group, self.block(0, 0) * CORES + 1 - self.core)


class Gather:
    def __init__(self, buf, sem, place, sends):
        self.buf, self.sem, self.place, self.sends = buf, sem, place, sends
        self.width = buf.shape[2] // 2

    def copy(self, index, dx, dz, h, dev):
        view = self.buf.at[self.place.block(dx, dz), :, pl.ds(h * self.width, self.width)]
        return pltpu.make_async_remote_copy(
            src_ref=view,
            dst_ref=view,
            send_sem=self.sem.at[0, index],
            recv_sem=self.sem.at[1, index],
            device_id=dev,
            device_id_type=MESH,
        )

    def go(self, *args):
        copy = self.copy(*args)
        copy.start()
        self.sends.append(copy)

    def wait(self, index, dx, dz, h):
        self.copy(index, dx, dz, h, self.place.dev(1, 0)).wait_recv()

    def start(self):
        up, down = self.place.dev(0, 1), self.place.dev(0, -1)
        self.go(0, 0, 0, 0, up)
        self.go(2, 0, 0, 1, down)
        self.go(1, 0, 0, 1, up)
        self.go(3, 0, 0, 0, down)
        self.x_near(0)

    def x_near(self, j):
        up, down = self.place.dev(1, 0), self.place.dev(-1, 0)
        base, dz = 6 + 6 * j, STEPS[j]
        self.go(base, 0, dz, 0, up)
        self.go(base + 2, 0, dz, 1, down)
        self.go(base + 1, 0, dz, 1, up)
        self.go(base + 3, 0, dz, 0, down)

    def z_forward(self):
        self.wait(0, 0, -1, 0)
        self.go(4, 0, -1, 0, self.place.dev(0, 1))
        self.wait(2, 0, 1, 1)
        self.go(5, 0, 1, 1, self.place.dev(0, -1))

    def z_near(self):
        self.wait(1, 0, -1, 1)
        self.x_near(1)
        self.wait(3, 0, 1, 0)
        self.x_near(2)

    def z_far(self, direct):
        up, down, opposite = self.place.dev(1, 0), self.place.dev(-1, 0), self.place.dev(2, 0)
        base = 6 + 6 * 3
        self.wait(4, 0, 2, 0)
        if direct:
            self.go(base + 4, 0, 2, 0, opposite)
        self.go(base, 0, 2, 0, up)
        self.go(base + 3, 0, 2, 0, down)
        self.wait(5, 0, 2, 1)
        if direct:
            self.go(base + 5, 0, 2, 1, opposite)
        self.go(base + 2, 0, 2, 1, down)
        self.go(base + 1, 0, 2, 1, up)

    def x_forward(self, j):
        base, dz = 6 + 6 * j, STEPS[j]
        self.wait(base, -1, dz, 0)
        self.go(base + 4, -1, dz, 0, self.place.dev(1, 0))
        self.wait(base + 2, 1, dz, 1)
        self.go(base + 5, 1, dz, 1, self.place.dev(-1, 0))

    def x_done(self, j, direct=False):
        base, dz = 6 + 6 * j, STEPS[j]
        if direct:
            self.wait(base, -1, dz, 0)
            self.wait(base + 2, 1, dz, 1)
        self.wait(base + 1, -1, dz, 1)
        self.wait(base + 3, 1, dz, 0)
        self.wait(base + 4, 2, dz, 0)
        self.wait(base + 5, 2, dz, 1)


def kernel(
    groups,
    teacher_rows_in,
    student_rows_in,
    teacher_gain_in,
    student_gain_in,
    teacher_head,
    student_head,
    route_in,
    target_in,
    loss_out,
    grad_out,
    teacher_rows,
    student_rows,
    teacher_gain,
    student_gain,
    route,
    target,
    head_t,
    head_s,
    rows_t,
    rows_s,
    wide,
    out_rows,
    in_rows,
    routed,
    hat_keep,
    inverse_keep,
    target_keep,
    logits_t,
    logits_s,
    exp_s,
    stat_all,
    columns_keep,
    part,
    xf_out,
    xf_in,
    xn_out,
    xn_in,
    z_part,
    zf_out,
    zf_in,
    zn_out,
    zn_in,
    local_sem,
    head_sem,
    route_sem,
    gather_t_sem,
    gather_s_sem,
    stat_sem,
    back_sem,
):
    p = Place()
    g, v, core = p.group, p.vocab, p.core
    f32, bf16 = jnp.float32, jnp.bfloat16
    local_rows, dt = teacher_rows.shape
    ds = student_rows.shape[1]
    shard = head_s.shape[2]
    ht, hs = dt // 2, ds // 2
    qs = hs // 2
    rows = BLOCKS * local_rows
    chunk = dt // SUB
    sends = []

    def remote(src, dst, sem, index, dev):
        copy = pltpu.make_async_remote_copy(
            src_ref=src,
            dst_ref=dst,
            send_sem=sem.at[0, index],
            recv_sem=sem.at[1, index],
            device_id=dev,
            device_id_type=MESH,
        )
        copy.start()
        sends.append(copy)
        return copy

    def fetch(src, dst, index):
        copy = pltpu.make_async_copy(src, dst, local_sem.at[index])
        copy.start()
        return copy

    barrier = pltpu.get_barrier_semaphore()

    def greet(dev):
        pl.semaphore_signal(barrier, inc=1, device_id=dev, device_id_type=MESH)

    for d in range(1, BLOCKS):
        greet(p.nth(d))
    greet(p.other())
    for d in range(1, groups):
        greet((lax.rem(g + d, groups), v))

    load_rows_s = fetch(student_rows_in, student_rows, 0)
    load_gain_s = fetch(student_gain_in, student_gain, 1)
    load_rows_t = fetch(teacher_rows_in, teacher_rows, 2)
    load_gain_t = fetch(teacher_gain_in, teacher_gain, 3)
    load_route = fetch(route_in, route, 4)
    load_target = fetch(target_in, target, 5)
    load_head_s = fetch(student_head, head_s.at[core], 6)
    load_head_t = fetch(teacher_head, head_t.at[core], 7)

    load_rows_s.wait()
    load_gain_s.wait()
    here = p.block(0, 0)
    wide_s = student_rows[...].astype(f32)
    inverse = lax.rsqrt(jnp.mean(wide_s * wide_s, axis=1, keepdims=True) + epsilon)
    inverse_keep[...] = jnp.broadcast_to(inverse, inverse_keep.shape)
    hat = wide_s * inverse
    hat_keep[...] = hat
    gain_s = student_gain[...].astype(f32).reshape(1, ds)
    normed_s = hat * gain_s
    rows_s[here] = jnp.concatenate([normed_s[:, :hs], normed_s[:, hs:]], axis=0).astype(bf16)

    pl.semaphore_wait(barrier, groups - 1 + BLOCKS - 1 + 1)

    student = Gather(rows_s, gather_s_sem, p, sends)
    teacher = Gather(rows_t, gather_t_sem, p, sends)
    student.start()

    load_rows_t.wait()
    load_gain_t.wait()
    load_route.wait()
    wide_t = teacher_rows[...].astype(f32)
    inverse_t = lax.rsqrt(jnp.mean(wide_t * wide_t, axis=1, keepdims=True) + epsilon)
    normed_t = wide_t * inverse_t * teacher_gain[...].astype(f32).reshape(1, dt)
    for c in range(SUB):
        wide[:, c, :] = normed_t[:, c * chunk : (c + 1) * chunk]
    span = lax.axis_size("vocab") * local_rows
    first = g * span + v * local_rows
    my_routes = [route[first + k] for k in range(local_rows)]

    @pl.loop(0, groups)
    def _(dest):
        total = jnp.zeros((SUB, chunk), f32)
        for k in range(local_rows):
            total += jnp.where(my_routes[k] == dest, 1.0, 0.0) * wide[k]
        out_rows[dest] = total.astype(bf16)

    in_rows[g] = out_rows[g]
    routed_copies = []
    for d in range(1, groups):
        dest = lax.rem(g + d, groups)
        routed_copies.append(
            remote(out_rows.at[dest], in_rows.at[g], route_sem, d, (dest, v))
        )
    fetch_head_s = remote(student_head, head_s.at[core], head_sem, 0, p.other())
    fetch_head_t = remote(teacher_head, head_t.at[core], head_sem, 1, p.other())

    student.z_forward()

    ranks, valids = [], []
    seen = jnp.int32(0)
    for t in range(groups):
        start = t * span + v * local_rows
        valid = jnp.int32(0)
        for k in range(local_rows):
            valid += jnp.where(route[start + k] == g, 1, 0)
        ranks.append(seen)
        valids.append(valid)
        seen = seen + valid
    for copy in routed_copies:
        copy.wait_recv()
    for j in range(local_rows):
        total = jnp.zeros((SUB, chunk), f32)
        for t in range(groups):
            weight = jnp.where(ranks[t] == j, valids[t], 0).astype(f32)
            total += weight * in_rows[t].astype(f32)
        wide[j] = total
    for c in range(SUB):
        half, at = divmod(c * chunk, ht)
        routed[half * 8 : half * 8 + 8, at : at + chunk] = wide[:, c, :]
    rows_t[here] = routed[...].astype(bf16)
    teacher.start()

    student.x_forward(0)
    student.z_near()
    teacher.x_forward(0)
    student.z_far(False)
    student.x_forward(1)
    student.x_forward(2)
    teacher.z_forward()
    student.x_forward(3)
    teacher.z_near()

    load_target.wait()
    all_targets = jnp.transpose(jnp.broadcast_to(target[...].astype(f32), (128, 2 * rows)))
    target_keep[...] = all_targets
    columns = (v // CORES) * (CORES * shard) + lax.broadcasted_iota(
        jnp.int32, (rows, CORES * shard), 1
    )
    my_targets = jnp.concatenate(
        [
            target_keep[pl.ds(pl.multiple_of(b * 16 + core * 8, 8), 8), :]
            for b in range(BLOCKS)
        ],
        axis=0,
    )[:, 0:1].astype(jnp.int32)

    def logits(left, count, head, half):
        parts = []
        for c in range(CORES):
            low = jnp.dot(left, head[c, 0:half, :], preferred_element_type=f32)
            high = jnp.dot(left, head[c, half : 2 * half, :], preferred_element_type=f32)
            low = low.reshape(count, 16, shard)[:, 0:8]
            high = high.reshape(count, 16, shard)[:, 8:16]
            parts.append((low + high).reshape(count * 8, shard))
        return jnp.concatenate(parts, axis=1)

    for j in range(RING):
        student.x_done(j)
    load_head_s.wait()
    fetch_head_s.wait_recv()
    values = logits(rows_s[...].reshape(BLOCKS * 16, hs), BLOCKS, head_s, hs)
    logits_s[...] = values
    top_s = jnp.max(values, axis=1, keepdims=True)
    powers = jnp.exp(values - top_s)
    exp_s[...] = powers
    sum_s = jnp.sum(powers, axis=1, keepdims=True)
    picked = jnp.sum(jnp.where(columns == my_targets, values, 0.0), axis=1, keepdims=True)

    teacher.x_forward(1)
    teacher.x_forward(2)
    teacher.z_far(True)

    def teacher_logits(steps):
        blocks = [p.block(dx, STEPS[j]) for j in steps for dx in range(RING)]
        left = jnp.concatenate([rows_t[b] for b in blocks], axis=0)
        values = logits(left, len(blocks), head_t, ht)
        for i, b in enumerate(blocks):
            logits_t[pl.ds(pl.multiple_of(b * 8, 8), 8), :] = values[i * 8 : i * 8 + 8]

    load_head_t.wait()
    fetch_head_t.wait_recv()
    for j in range(3):
        teacher.x_done(j)
    teacher_logits((0, 1, 2))
    teacher.x_done(3, True)
    teacher_logits((3,))

    values = logits_t[...]
    top_t = jnp.max(values, axis=1, keepdims=True)
    exp_t = jnp.exp(values - top_t)
    sum_t = jnp.sum(exp_t, axis=1, keepdims=True)
    cross = jnp.sum(exp_t * (values - logits_s[...]), axis=1, keepdims=True)

    lane = lax.broadcasted_iota(jnp.int32, (rows, 128), 1)
    packed = jnp.zeros((rows, 128), f32)
    for i, value in enumerate((top_t, top_s, top_t, None, sum_t, sum_s, cross, picked)):
        if value is not None:
            packed = jnp.where(lane == i, value, packed)
    stats = jnp.transpose(packed)[0:8, :]

    stat_all[here] = stats
    copies = [
        remote(stat_all.at[here], stat_all.at[here], stat_sem, d, p.nth(d))
        for d in range(1, BLOCKS)
    ]
    for copy in copies:
        copy.wait_recv()
    parts = [stat_all[i] for i in range(BLOCKS)]
    tops = functools.reduce(jnp.maximum, [part[0:4] for part in parts])
    sums = sum(jnp.exp(part[0:4] - tops) * part[4:8] for part in parts)
    merged = jnp.concatenate([tops, sums], axis=0)
    all_top_t, all_top_s = merged[0:1], merged[1:2]
    all_sum_t, all_sum_s = merged[4:5], merged[5:6]
    scale_t = (loss_scale * distill_mix) * jnp.exp(stats[0:1] - all_top_t) / all_sum_t
    scale_s = loss_scale * jnp.exp(stats[1:2] - all_top_s) / all_sum_s
    lse_t = all_top_t + jnp.log(all_sum_t)
    lse_s = all_top_s + jnp.log(all_sum_s)
    loss = distill_mix * (merged[6:7] / all_sum_t - lse_t + lse_s) + (1.0 - distill_mix) * (
        lse_s - merged[7:8]
    )
    turned = jnp.transpose(
        jnp.concatenate([scale_t, scale_s, loss, jnp.zeros((125, rows), f32)], axis=0)
    )
    columns_keep[core] = turned
    loss_copy = remote(columns_keep.at[core], columns_keep.at[core], head_sem, 2, p.other())
    logit_grad = (
        exp_s[...] * turned[:, 1:2]
        - exp_t * turned[:, 0:1]
        - jnp.where(columns == my_targets, loss_scale * (1.0 - distill_mix), 0.0)
    ).astype(bf16)

    step = qs // 2
    for n in range(ds // step):
        half, at = divmod(n * step, hs)
        block = contract_last(
            logit_grad[:, 0:shard], head_s[0, n * step : (n + 1) * step, :]
        ) + contract_last(logit_grad[:, shard:], head_s[1, n * step : (n + 1) * step, :])
        part[:, half * 8 : half * 8 + 8, at : at + step] = block.reshape(
            BLOCKS, local_rows, step
        )

    order = (2, 1, -1, 0)
    plus_x, minus_x = p.dev(1, 0), p.dev(-1, 0)
    plus_z, minus_z = p.dev(0, 1), p.dev(0, -1)
    cols = (slice(0, qs), slice(qs, hs))
    far_copies, near_copies = {}, {}

    def x_first(i):
        far, up, down = (part.at[p.block(d, order[i])] for d in (2, 1, -1))
        xf_out[i, 0] = far[:, cols[0]].astype(bf16)
        xf_out[i, 1] = far[:, cols[1]].astype(bf16)
        far_copies[i] = (
            remote(xf_out.at[i, 0], xf_in.at[i, 0], back_sem, 2 * i, plus_x),
            remote(xf_out.at[i, 1], xf_in.at[i, 1], back_sem, 1 + 2 * i, minus_x),
        )
        xn_out[i, 0, 1] = up[:, cols[1]].astype(bf16)
        xn_out[i, 1, 0] = down[:, cols[0]].astype(bf16)
        near_copies[i] = [
            remote(xn_out.at[i, 0, 1], xn_in.at[i, 0, 1], back_sem, 8 + 2 * i, plus_x),
            remote(xn_out.at[i, 1, 0], xn_in.at[i, 1, 0], back_sem, 9 + 2 * i, minus_x),
        ]

    def x_second(i):
        up, down = (part.at[p.block(d, order[i])] for d in (1, -1))
        far_copies[i][0].wait_recv()
        xn_out[i, 0, 0] = (up[:, cols[0]] + xf_in[i, 0].astype(f32)).astype(bf16)
        near_copies[i].append(
            remote(xn_out.at[i, 0, 0], xn_in.at[i, 0, 0], back_sem, 16 + 2 * i, plus_x)
        )
        far_copies[i][1].wait_recv()
        xn_out[i, 1, 1] = (down[:, cols[1]] + xf_in[i, 1].astype(f32)).astype(bf16)
        near_copies[i].append(
            remote(xn_out.at[i, 1, 1], xn_in.at[i, 1, 1], back_sem, 17 + 2 * i, minus_x)
        )

    def x_done(i):
        for copy in near_copies[i]:
            copy.wait_recv()
        block = part.at[p.block(0, order[i])]
        return [
            block[:, cols[h]] + xn_in[i, 0, h].astype(f32) + xn_in[i, 1, h].astype(f32)
            for h in range(2)
        ]

    x_first(0)
    x_first(1)
    x_second(0)
    x_first(2)
    x_second(1)
    x_first(3)
    x_second(2)
    z_far = []
    for h, value in enumerate(x_done(0)):
        zf_out[h] = value.astype(bf16)
        z_far.append(
            remote(zf_out.at[h], zf_in.at[h], back_sem, 24 + h, (plus_z, minus_z)[h])
        )
    x_second(3)
    up = x_done(1)
    zn_out[0, 1] = up[1].astype(bf16)
    z_near = [remote(zn_out.at[0, 1], zn_in.at[0, 1], back_sem, 26, plus_z)]
    z_part[0] = up[0]
    down = x_done(2)
    zn_out[1, 0] = down[0].astype(bf16)
    z_near.append(remote(zn_out.at[1, 0], zn_in.at[1, 0], back_sem, 27, minus_z))
    z_part[1] = down[1]
    z_far[0].wait_recv()
    zn_out[0, 0] = (z_part[0] + zf_in[0].astype(f32)).astype(bf16)
    z_near.append(remote(zn_out.at[0, 0], zn_in.at[0, 0], back_sem, 28, plus_z))
    z_far[1].wait_recv()
    zn_out[1, 1] = (z_part[1] + zf_in[1].astype(f32)).astype(bf16)
    z_near.append(remote(zn_out.at[1, 1], zn_in.at[1, 1], back_sem, 29, minus_z))
    for h, value in enumerate(x_done(3)):
        z_part[2 + h] = value

    loss_copy.wait_recv()
    both = jnp.concatenate(
        [columns_keep[c, b * 8 : b * 8 + 8, :] for b in range(BLOCKS) for c in range(CORES)],
        axis=0,
    )
    loss_out[...] = jnp.transpose(both)[2:3, :]
    inverse = inverse_keep[:, 0:1]
    hat = hat_keep[...]
    gain = student_gain[...].astype(f32).reshape(1, ds)

    for copy in z_near:
        copy.wait_recv()
    mine = [
        z_part[2 + h] + zn_in[0, h].astype(f32) + zn_in[1, h].astype(f32) for h in range(2)
    ]
    scaled = (
        jnp.concatenate([mine[0][0:8], mine[1][0:8], mine[0][8:16], mine[1][8:16]], axis=1)
        * gain
    )
    grad_out[...] = (
        inverse * (scaled - hat * jnp.mean(scaled * hat, axis=1, keepdims=True))
    ).astype(bf16)

    for copy in sends:
        copy.wait_send()


def local(
    teacher_rows,
    student_rows,
    teacher_gain,
    student_gain,
    teacher_head,
    student_head,
    route,
    target,
):
    groups = lax.axis_size("group")
    f32, bf16 = jnp.float32, jnp.bfloat16
    local_rows, dt = teacher_rows.shape
    ds = student_rows.shape[1]
    shard = teacher_head.shape[1]
    all_rows = target.shape[0]
    rows = all_rows // CORES
    ht, hs = dt // 2, ds // 2
    qs, chunk = hs // 2, dt // SUB
    vmem = pl.BlockSpec(memory_space=pltpu.VMEM)
    anywhere = pl.BlockSpec(memory_space=pl.ANY)
    loss, grad = pl.pallas_call(
        functools.partial(kernel, groups),
        out_shape=(
            jax.ShapeDtypeStruct((1, all_rows), f32),
            jax.ShapeDtypeStruct((local_rows, ds), bf16),
        ),
        in_specs=[anywhere] * 8,
        out_specs=(vmem, vmem),
        scratch_shapes=[
            pltpu.VMEM((local_rows, dt), bf16),
            pltpu.VMEM((local_rows, ds), bf16),
            pltpu.VMEM((dt,), bf16),
            pltpu.VMEM((ds,), bf16),
            pltpu.SMEM(route.shape, jnp.int32),
            pltpu.VMEM((1, all_rows), jnp.int32),
            pltpu.VMEM((CORES, dt, shard), bf16),
            pltpu.VMEM((CORES, ds, shard), bf16),
            pltpu.VMEM((BLOCKS, 16, ht), bf16),
            pltpu.VMEM((BLOCKS, 16, hs), bf16),
            pltpu.VMEM((local_rows, SUB, chunk), f32),
            pltpu.VMEM((groups, SUB, chunk), bf16),
            pltpu.VMEM((groups, SUB, chunk), bf16),
            pltpu.VMEM((16, ht), f32),
            pltpu.VMEM((local_rows, ds), f32),
            pltpu.VMEM((local_rows, 128), f32),
            pltpu.VMEM((all_rows, 128), f32),
            pltpu.VMEM((rows, CORES * shard), f32),
            pltpu.VMEM((rows, CORES * shard), f32),
            pltpu.VMEM((rows, CORES * shard), f32),
            pltpu.VMEM((BLOCKS, 8, rows), f32),
            pltpu.VMEM((CORES, rows, 128), f32),
            pltpu.VMEM((BLOCKS, 16, hs), f32),
            pltpu.VMEM((4, 2, 16, qs), bf16),
            pltpu.VMEM((4, 2, 16, qs), bf16),
            pltpu.VMEM((4, 2, 2, 16, qs), bf16),
            pltpu.VMEM((4, 2, 2, 16, qs), bf16),
            pltpu.VMEM((4, 16, qs), f32),
            pltpu.VMEM((2, 16, qs), bf16),
            pltpu.VMEM((2, 16, qs), bf16),
            pltpu.VMEM((2, 2, 16, qs), bf16),
            pltpu.VMEM((2, 2, 16, qs), bf16),
            pltpu.SemaphoreType.DMA((8,)),
            pltpu.SemaphoreType.DMA((2, 3)),
            pltpu.SemaphoreType.DMA((2, groups)),
            pltpu.SemaphoreType.DMA((2, GATHER_COPIES)),
            pltpu.SemaphoreType.DMA((2, GATHER_COPIES)),
            pltpu.SemaphoreType.DMA((2, BLOCKS)),
            pltpu.SemaphoreType.DMA((2, 30)),
        ],
        compiler_params=pltpu.CompilerParams(
            collective_id=0, has_side_effects=True, vmem_limit_bytes=60 * 1024 * 1024
        ),
        name="distill",
    )(
        teacher_rows,
        student_rows,
        teacher_gain,
        student_gain,
        teacher_head,
        student_head,
        route,
        target.reshape(1, all_rows),
    )
    return (loss.reshape(all_rows), grad)


def solution(mesh):
    placed = (
        P(("group", "vocab"), None),
        P(("group", "vocab"), None),
        P(),
        P(),
        P(None, "vocab"),
        P(None, "vocab"),
        P(),
        P("group"),
    )
    return jax.shard_map(
        local,
        mesh=mesh,
        in_specs=placed,
        out_specs=(P("group"), P(("group", "vocab"), None)),
        check_vma=False,
    )
```

```python
import functools

import jax
import jax.numpy as jnp
from jax import lax
from jax.experimental import pallas as pl
from jax.experimental.pallas import tpu as pltpu
from jax.sharding import PartitionSpec as P

MESH = pl.DeviceIdType.MESH
epsilon = 1e-06
loss_scale = 16.0
distill_mix = 0.5

RING = 4
CORES = 2
BLOCKS = RING * RING
SUB = 16
STEPS = (0, -1, 1, 2)
GATHER_COPIES = 6 + 6 * RING


def contract_last(left_side, right_side):
    return lax.dot_general(
        left_side, right_side, (((1,), (1,)), ((), ())), preferred_element_type=jnp.float32
    )


class Place:
    def __init__(self):
        self.group = lax.axis_index("group")
        self.vocab = lax.axis_index("vocab")
        self.core = lax.rem(self.vocab, CORES)
        self.zh = lax.rem(self.vocab // CORES, RING)
        self.x = self.vocab // (CORES * RING)

    def block(self, dx, dz):
        xx, zz = lax.rem(self.x + dx + RING, RING), lax.rem(self.zh + dz + RING, RING)
        return xx * RING + zz

    def dev(self, dx, dz):
        return (self.group, self.block(dx, dz) * CORES + self.core)

    def nth(self, d):
        return (self.group, lax.rem(self.block(0, 0) + d, BLOCKS) * CORES + self.core)

    def other(self):
        return (self.group, self.block(0, 0) * CORES + 1 - self.core)


class Gather:
    def __init__(self, buf, sem, place, sends):
        self.buf, self.sem, self.place, self.sends = buf, sem, place, sends
        self.width = buf.shape[2] // 2

    def copy(self, index, dx, dz, h, dev):
        view = self.buf.at[self.place.block(dx, dz), :, pl.ds(h * self.width, self.width)]
        return pltpu.make_async_remote_copy(
            src_ref=view,
            dst_ref=view,
            send_sem=self.sem.at[0, index],
            recv_sem=self.sem.at[1, index],
            device_id=dev,
            device_id_type=MESH,
        )

    def go(self, *args):
        copy = self.copy(*args)
        copy.start()
        self.sends.append(copy)

    def wait(self, index, dx, dz, h):
        self.copy(index, dx, dz, h, self.place.dev(1, 0)).wait_recv()

    def start(self):
        up, down = self.place.dev(0, 1), self.place.dev(0, -1)
        self.go(0, 0, 0, 0, up)
        self.go(2, 0, 0, 1, down)
        self.go(1, 0, 0, 1, up)
        self.go(3, 0, 0, 0, down)
        self.x_half(0, 0)
        self.x_half(0, 1)

    def x_half(self, j, h):
        up, down = self.place.dev(1, 0), self.place.dev(-1, 0)
        base, dz = 6 + 6 * j, STEPS[j]
        if h == 0:
            self.go(base, 0, dz, 0, up)
            self.go(base + 3, 0, dz, 0, down)
        else:
            self.go(base + 2, 0, dz, 1, down)
            self.go(base + 1, 0, dz, 1, up)

    def z_forward(self):
        self.wait(0, 0, -1, 0)
        self.go(4, 0, -1, 0, self.place.dev(0, 1))
        self.x_half(1, 0)
        self.wait(2, 0, 1, 1)
        self.go(5, 0, 1, 1, self.place.dev(0, -1))
        self.x_half(2, 1)

    def z_near(self):
        self.wait(1, 0, -1, 1)
        self.x_half(1, 1)
        self.wait(3, 0, 1, 0)
        self.x_half(2, 0)

    def z_far(self, direct):
        up, down, opposite = self.place.dev(1, 0), self.place.dev(-1, 0), self.place.dev(2, 0)
        base = 6 + 6 * 3
        self.wait(4, 0, 2, 0)
        if direct:
            self.go(base + 4, 0, 2, 0, opposite)
        self.go(base, 0, 2, 0, up)
        self.go(base + 3, 0, 2, 0, down)
        self.wait(5, 0, 2, 1)
        if direct:
            self.go(base + 5, 0, 2, 1, opposite)
        self.go(base + 2, 0, 2, 1, down)
        self.go(base + 1, 0, 2, 1, up)

    def x_forward(self, j):
        base, dz = 6 + 6 * j, STEPS[j]
        self.wait(base, -1, dz, 0)
        self.go(base + 4, -1, dz, 0, self.place.dev(1, 0))
        self.wait(base + 2, 1, dz, 1)
        self.go(base + 5, 1, dz, 1, self.place.dev(-1, 0))

    def x_done(self, j, direct=False):
        base, dz = 6 + 6 * j, STEPS[j]
        if direct:
            self.wait(base, -1, dz, 0)
            self.wait(base + 2, 1, dz, 1)
        self.wait(base + 1, -1, dz, 1)
        self.wait(base + 3, 1, dz, 0)
        self.wait(base + 4, 2, dz, 0)
        self.wait(base + 5, 2, dz, 1)


def kernel(
    groups,
    teacher_rows_in,
    student_rows_in,
    teacher_gain_in,
    student_gain_in,
    teacher_head,
    student_head,
    route_in,
    target_in,
    loss_out,
    grad_out,
    teacher_rows,
    student_rows,
    teacher_gain,
    student_gain,
    route,
    target,
    head_t,
    head_s,
    rows_t,
    rows_s,
    wide,
    out_rows,
    in_rows,
    routed,
    hat_keep,
    inverse_keep,
    target_keep,
    logits_t,
    logits_s,
    exp_s,
    stat_all,
    columns_keep,
    part,
    xf_out,
    xf_in,
    xn_out,
    xn_in,
    z_part,
    zf_out,
    zf_in,
    zn_out,
    zn_in,
    local_sem,
    head_sem,
    route_sem,
    gather_t_sem,
    gather_s_sem,
    stat_sem,
    back_sem,
):
    p = Place()
    g, v, core = p.group, p.vocab, p.core
    f32, bf16 = jnp.float32, jnp.bfloat16
    local_rows, dt = teacher_rows.shape
    ds = student_rows.shape[1]
    shard = head_s.shape[2]
    ht, hs = dt // 2, ds // 2
    qs = hs // 2
    rows = BLOCKS * local_rows
    chunk = dt // SUB
    sends = []

    def remote(src, dst, sem, index, dev):
        copy = pltpu.make_async_remote_copy(
            src_ref=src,
            dst_ref=dst,
            send_sem=sem.at[0, index],
            recv_sem=sem.at[1, index],
            device_id=dev,
            device_id_type=MESH,
        )
        copy.start()
        sends.append(copy)
        return copy

    def fetch(src, dst, index):
        copy = pltpu.make_async_copy(src, dst, local_sem.at[index])
        copy.start()
        return copy

    barrier = pltpu.get_barrier_semaphore()

    def greet(dev):
        pl.semaphore_signal(barrier, inc=1, device_id=dev, device_id_type=MESH)

    load_rows_s = fetch(student_rows_in, student_rows, 0)
    load_gain_s = fetch(student_gain_in, student_gain, 1)
    load_rows_t = fetch(teacher_rows_in, teacher_rows, 2)
    load_gain_t = fetch(teacher_gain_in, teacher_gain, 3)
    load_route = fetch(route_in, route, 4)
    load_target = fetch(target_in, target, 5)
    load_head_s = fetch(student_head, head_s.at[core], 6)
    load_head_t = fetch(teacher_head, head_t.at[core], 7)
    for d in range(1, RING):
        greet(p.dev(d, 0))
    greet(p.dev(0, 1))
    greet(p.dev(0, -1))
    greet(p.other())
    for d in range(1, groups):
        greet((lax.rem(g + d, groups), v))

    load_rows_s.wait()
    load_gain_s.wait()
    here = p.block(0, 0)
    wide_s = student_rows[...].astype(f32)
    inverse = lax.rsqrt(jnp.mean(wide_s * wide_s, axis=1, keepdims=True) + epsilon)
    inverse_keep[...] = jnp.broadcast_to(inverse, inverse_keep.shape)
    hat = wide_s * inverse
    hat_keep[...] = hat
    gain_s = student_gain[...].astype(f32).reshape(1, ds)
    normed_s = hat * gain_s
    rows_s[here] = jnp.concatenate([normed_s[:, :hs], normed_s[:, hs:]], axis=0).astype(bf16)

    pl.semaphore_wait(barrier, groups - 1 + RING - 1 + 2 + 1)

    student = Gather(rows_s, gather_s_sem, p, sends)
    teacher = Gather(rows_t, gather_t_sem, p, sends)
    student.start()

    load_rows_t.wait()
    load_gain_t.wait()
    load_route.wait()
    wide_t = teacher_rows[...].astype(f32)
    inverse_t = lax.rsqrt(jnp.mean(wide_t * wide_t, axis=1, keepdims=True) + epsilon)
    normed_t = wide_t * inverse_t * teacher_gain[...].astype(f32).reshape(1, dt)
    for c in range(SUB):
        wide[:, c, :] = normed_t[:, c * chunk : (c + 1) * chunk]
    span = lax.axis_size("vocab") * local_rows
    first = g * span + v * local_rows
    my_routes = [route[first + k] for k in range(local_rows)]

    @pl.loop(0, groups)
    def _(dest):
        total = jnp.zeros((SUB, chunk), f32)
        for k in range(local_rows):
            total += jnp.where(my_routes[k] == dest, 1.0, 0.0) * wide[k]
        out_rows[dest] = total.astype(bf16)

    in_rows[g] = out_rows[g]
    routed_copies = []
    for d in range(1, groups):
        dest = lax.rem(g + d, groups)
        routed_copies.append(
            remote(out_rows.at[dest], in_rows.at[g], route_sem, d, (dest, v))
        )
    fetch_head_s = remote(student_head, head_s.at[core], head_sem, 0, p.other())
    fetch_head_t = remote(teacher_head, head_t.at[core], head_sem, 1, p.other())

    student.z_forward()

    ranks, valids = [], []
    seen = jnp.int32(0)
    for t in range(groups):
        start = t * span + v * local_rows
        valid = jnp.int32(0)
        for k in range(local_rows):
            valid += jnp.where(route[start + k] == g, 1, 0)
        ranks.append(seen)
        valids.append(valid)
        seen = seen + valid
    for copy in routed_copies:
        copy.wait_recv()
    for j in range(local_rows):
        total = jnp.zeros((SUB, chunk), f32)
        for t in range(groups):
            weight = jnp.where(ranks[t] == j, valids[t], 0).astype(f32)
            total += weight * in_rows[t].astype(f32)
        wide[j] = total
    for c in range(SUB):
        half, at = divmod(c * chunk, ht)
        routed[half * 8 : half * 8 + 8, at : at + chunk] = wide[:, c, :]
    rows_t[here] = routed[...].astype(bf16)
    teacher.start()

    student.x_forward(0)
    student.z_near()
    teacher.x_forward(0)
    student.z_far(False)
    student.x_forward(1)
    student.x_forward(2)
    teacher.z_forward()
    student.x_forward(3)
    teacher.z_near()

    load_target.wait()
    all_targets = jnp.transpose(jnp.broadcast_to(target[...].astype(f32), (128, 2 * rows)))
    target_keep[...] = all_targets
    columns = (v // CORES) * (CORES * shard) + lax.broadcasted_iota(
        jnp.int32, (rows, CORES * shard), 1
    )
    my_targets = jnp.concatenate(
        [
            target_keep[pl.ds(pl.multiple_of(b * 16 + core * 8, 8), 8), :]
            for b in range(BLOCKS)
        ],
        axis=0,
    )[:, 0:1].astype(jnp.int32)

    def logits(left, count, head, half):
        parts = []
        for c in range(CORES):
            low = jnp.dot(left, head[c, 0:half, :], preferred_element_type=f32)
            high = jnp.dot(left, head[c, half : 2 * half, :], preferred_element_type=f32)
            low = low.reshape(count, 16, shard)[:, 0:8]
            high = high.reshape(count, 16, shard)[:, 8:16]
            parts.append((low + high).reshape(count * 8, shard))
        return jnp.concatenate(parts, axis=1)

    teacher.x_forward(1)
    teacher.x_forward(2)
    teacher.z_far(True)
    for j in range(RING):
        student.x_done(j)
    load_head_s.wait()
    fetch_head_s.wait_recv()
    values = logits(rows_s[...].reshape(BLOCKS * 16, hs), BLOCKS, head_s, hs)
    logits_s[...] = values
    top_s = jnp.max(values, axis=1, keepdims=True)
    powers = jnp.exp(values - top_s)
    exp_s[...] = powers
    sum_s = jnp.sum(powers, axis=1, keepdims=True)
    picked = jnp.sum(jnp.where(columns == my_targets, values, 0.0), axis=1, keepdims=True)


    def teacher_logits(steps):
        blocks = [p.block(dx, STEPS[j]) for j in steps for dx in range(RING)]
        left = jnp.concatenate([rows_t[b] for b in blocks], axis=0)
        values = logits(left, len(blocks), head_t, ht)
        for i, b in enumerate(blocks):
            logits_t[pl.ds(pl.multiple_of(b * 8, 8), 8), :] = values[i * 8 : i * 8 + 8]

    load_head_t.wait()
    fetch_head_t.wait_recv()
    for j in range(3):
        teacher.x_done(j)
    teacher_logits((0, 1, 2))
    teacher.x_done(3, True)
    teacher_logits((3,))

    values = logits_t[...]
    top_t = jnp.max(values, axis=1, keepdims=True)
    exp_t = jnp.exp(values - top_t)
    sum_t = jnp.sum(exp_t, axis=1, keepdims=True)
    cross = jnp.sum(exp_t * (values - logits_s[...]), axis=1, keepdims=True)

    lane = lax.broadcasted_iota(jnp.int32, (rows, 128), 1)
    packed = jnp.zeros((rows, 128), f32)
    for i, value in enumerate((top_t, top_s, top_t, None, sum_t, sum_s, cross, picked)):
        if value is not None:
            packed = jnp.where(lane == i, value, packed)
    stats = jnp.transpose(packed)[0:8, :]

    stat_all[here] = stats
    copies = [
        remote(stat_all.at[here], stat_all.at[here], stat_sem, d, p.nth(d))
        for d in range(1, BLOCKS)
    ]
    for copy in copies:
        copy.wait_recv()
    parts = [stat_all[i] for i in range(BLOCKS)]
    tops = functools.reduce(jnp.maximum, [part[0:4] for part in parts])
    sums = sum(jnp.exp(part[0:4] - tops) * part[4:8] for part in parts)
    merged = jnp.concatenate([tops, sums], axis=0)
    all_top_t, all_top_s = merged[0:1], merged[1:2]
    all_sum_t, all_sum_s = merged[4:5], merged[5:6]
    scale_t = (loss_scale * distill_mix) * jnp.exp(stats[0:1] - all_top_t) / all_sum_t
    scale_s = loss_scale * jnp.exp(stats[1:2] - all_top_s) / all_sum_s
    lse_t = all_top_t + jnp.log(all_sum_t)
    lse_s = all_top_s + jnp.log(all_sum_s)
    loss = distill_mix * (merged[6:7] / all_sum_t - lse_t + lse_s) + (1.0 - distill_mix) * (
        lse_s - merged[7:8]
    )
    turned = jnp.transpose(
        jnp.concatenate([scale_t, scale_s, loss, jnp.zeros((125, rows), f32)], axis=0)
    )
    columns_keep[core] = turned
    loss_copy = remote(columns_keep.at[core], columns_keep.at[core], head_sem, 2, p.other())
    logit_grad = (
        exp_s[...] * turned[:, 1:2]
        - exp_t * turned[:, 0:1]
        - jnp.where(columns == my_targets, loss_scale * (1.0 - distill_mix), 0.0)
    ).astype(bf16)

    step = qs // 2
    for n in range(ds // step):
        half, at = divmod(n * step, hs)
        block = contract_last(
            logit_grad[:, 0:shard], head_s[0, n * step : (n + 1) * step, :]
        ) + contract_last(logit_grad[:, shard:], head_s[1, n * step : (n + 1) * step, :])
        part[:, half * 8 : half * 8 + 8, at : at + step] = block.reshape(
            BLOCKS, local_rows, step
        )

    order = (2, 1, -1, 0)
    plus_x, minus_x = p.dev(1, 0), p.dev(-1, 0)
    plus_z, minus_z = p.dev(0, 1), p.dev(0, -1)
    cols = (slice(0, qs), slice(qs, hs))
    far_copies, near_copies = {}, {}

    def x_first(i):
        far, up, down = (part.at[p.block(d, order[i])] for d in (2, 1, -1))
        xf_out[i, 0] = far[:, cols[0]].astype(bf16)
        xf_out[i, 1] = far[:, cols[1]].astype(bf16)
        far_copies[i] = (
            remote(xf_out.at[i, 0], xf_in.at[i, 0], back_sem, 2 * i, plus_x),
            remote(xf_out.at[i, 1], xf_in.at[i, 1], back_sem, 1 + 2 * i, minus_x),
        )
        xn_out[i, 0, 1] = up[:, cols[1]].astype(bf16)
        xn_out[i, 1, 0] = down[:, cols[0]].astype(bf16)
        near_copies[i] = [
            remote(xn_out.at[i, 0, 1], xn_in.at[i, 0, 1], back_sem, 8 + 2 * i, plus_x),
            remote(xn_out.at[i, 1, 0], xn_in.at[i, 1, 0], back_sem, 9 + 2 * i, minus_x),
        ]

    def x_whole(i):
        slots = (xf_out.at[i], xn_out.at[i, 0], xn_out.at[i, 1])
        for slot, d in zip(slots, (2, 1, -1)):
            block = part.at[p.block(d, order[i])]
            for h in range(2):
                slot[h] = block[:, cols[h]].astype(bf16)
        near_copies[i] = [
            remote(slots[0], xf_in.at[i], back_sem, 2 * i, p.dev(2, 0)),
            remote(slots[1], xn_in.at[i, 0], back_sem, 8 + 2 * i, plus_x),
            remote(slots[2], xn_in.at[i, 1], back_sem, 9 + 2 * i, minus_x),
        ]

    def x_second(i):
        up, down = (part.at[p.block(d, order[i])] for d in (1, -1))
        far_copies[i][0].wait_recv()
        xn_out[i, 0, 0] = (up[:, cols[0]] + xf_in[i, 0].astype(f32)).astype(bf16)
        near_copies[i].append(
            remote(xn_out.at[i, 0, 0], xn_in.at[i, 0, 0], back_sem, 16 + 2 * i, plus_x)
        )
        far_copies[i][1].wait_recv()
        xn_out[i, 1, 1] = (down[:, cols[1]] + xf_in[i, 1].astype(f32)).astype(bf16)
        near_copies[i].append(
            remote(xn_out.at[i, 1, 1], xn_in.at[i, 1, 1], back_sem, 17 + 2 * i, minus_x)
        )

    def x_done(i):
        for copy in near_copies[i]:
            copy.wait_recv()
        block = part.at[p.block(0, order[i])]
        return [
            block[:, cols[h]] + xn_in[i, 0, h].astype(f32) + xn_in[i, 1, h].astype(f32)
            for h in range(2)
        ]

    x_whole(0)
    x_first(1)
    x_first(2)
    x_first(3)
    x_second(1)
    x_second(2)
    z_far = []
    for h, value in enumerate(x_done(0)):
        zf_out[h] = (value + xf_in[0, h].astype(f32)).astype(bf16)
        z_far.append(
            remote(zf_out.at[h], zf_in.at[h], back_sem, 24 + h, (plus_z, minus_z)[h])
        )
    x_second(3)
    up = x_done(1)
    zn_out[0, 1] = up[1].astype(bf16)
    z_near = [remote(zn_out.at[0, 1], zn_in.at[0, 1], back_sem, 26, plus_z)]
    z_part[0] = up[0]
    down = x_done(2)
    zn_out[1, 0] = down[0].astype(bf16)
    z_near.append(remote(zn_out.at[1, 0], zn_in.at[1, 0], back_sem, 27, minus_z))
    z_part[1] = down[1]
    z_far[0].wait_recv()
    zn_out[0, 0] = (z_part[0] + zf_in[0].astype(f32)).astype(bf16)
    z_near.append(remote(zn_out.at[0, 0], zn_in.at[0, 0], back_sem, 28, plus_z))
    z_far[1].wait_recv()
    zn_out[1, 1] = (z_part[1] + zf_in[1].astype(f32)).astype(bf16)
    z_near.append(remote(zn_out.at[1, 1], zn_in.at[1, 1], back_sem, 29, minus_z))
    for h, value in enumerate(x_done(3)):
        z_part[2 + h] = value

    loss_copy.wait_recv()
    both = jnp.concatenate(
        [columns_keep[c, b * 8 : b * 8 + 8, :] for b in range(BLOCKS) for c in range(CORES)],
        axis=0,
    )
    loss_out[...] = jnp.transpose(both)[2:3, :]
    inverse = inverse_keep[:, 0:1]
    hat = hat_keep[...]
    gain = student_gain[...].astype(f32).reshape(1, ds)

    for copy in z_near:
        copy.wait_recv()
    mine = [
        z_part[2 + h] + zn_in[0, h].astype(f32) + zn_in[1, h].astype(f32) for h in range(2)
    ]
    scaled = (
        jnp.concatenate([mine[0][0:8], mine[1][0:8], mine[0][8:16], mine[1][8:16]], axis=1)
        * gain
    )
    grad_out[...] = (
        inverse * (scaled - hat * jnp.mean(scaled * hat, axis=1, keepdims=True))
    ).astype(bf16)

    for copy in sends:
        copy.wait_send()


def local(
    teacher_rows,
    student_rows,
    teacher_gain,
    student_gain,
    teacher_head,
    student_head,
    route,
    target,
):
    groups = lax.axis_size("group")
    f32, bf16 = jnp.float32, jnp.bfloat16
    local_rows, dt = teacher_rows.shape
    ds = student_rows.shape[1]
    shard = teacher_head.shape[1]
    all_rows = target.shape[0]
    rows = all_rows // CORES
    ht, hs = dt // 2, ds // 2
    qs, chunk = hs // 2, dt // SUB
    vmem = pl.BlockSpec(memory_space=pltpu.VMEM)
    anywhere = pl.BlockSpec(memory_space=pl.ANY)
    loss, grad = pl.pallas_call(
        functools.partial(kernel, groups),
        out_shape=(
            jax.ShapeDtypeStruct((1, all_rows), f32),
            jax.ShapeDtypeStruct((local_rows, ds), bf16),
        ),
        in_specs=[anywhere] * 8,
        out_specs=(vmem, vmem),
        scratch_shapes=[
            pltpu.VMEM((local_rows, dt), bf16),
            pltpu.VMEM((local_rows, ds), bf16),
            pltpu.VMEM((dt,), bf16),
            pltpu.VMEM((ds,), bf16),
            pltpu.SMEM(route.shape, jnp.int32),
            pltpu.VMEM((1, all_rows), jnp.int32),
            pltpu.VMEM((CORES, dt, shard), bf16),
            pltpu.VMEM((CORES, ds, shard), bf16),
            pltpu.VMEM((BLOCKS, 16, ht), bf16),
            pltpu.VMEM((BLOCKS, 16, hs), bf16),
            pltpu.VMEM((local_rows, SUB, chunk), f32),
            pltpu.VMEM((groups, SUB, chunk), bf16),
            pltpu.VMEM((groups, SUB, chunk), bf16),
            pltpu.VMEM((16, ht), f32),
            pltpu.VMEM((local_rows, ds), f32),
            pltpu.VMEM((local_rows, 128), f32),
            pltpu.VMEM((all_rows, 128), f32),
            pltpu.VMEM((rows, CORES * shard), f32),
            pltpu.VMEM((rows, CORES * shard), f32),
            pltpu.VMEM((rows, CORES * shard), f32),
            pltpu.VMEM((BLOCKS, 8, rows), f32),
            pltpu.VMEM((CORES, rows, 128), f32),
            pltpu.VMEM((BLOCKS, 16, hs), f32),
            pltpu.VMEM((4, 2, 16, qs), bf16),
            pltpu.VMEM((4, 2, 16, qs), bf16),
            pltpu.VMEM((4, 2, 2, 16, qs), bf16),
            pltpu.VMEM((4, 2, 2, 16, qs), bf16),
            pltpu.VMEM((4, 16, qs), f32),
            pltpu.VMEM((2, 16, qs), bf16),
            pltpu.VMEM((2, 16, qs), bf16),
            pltpu.VMEM((2, 2, 16, qs), bf16),
            pltpu.VMEM((2, 2, 16, qs), bf16),
            pltpu.SemaphoreType.DMA((8,)),
            pltpu.SemaphoreType.DMA((2, 3)),
            pltpu.SemaphoreType.DMA((2, groups)),
            pltpu.SemaphoreType.DMA((2, GATHER_COPIES)),
            pltpu.SemaphoreType.DMA((2, GATHER_COPIES)),
            pltpu.SemaphoreType.DMA((2, BLOCKS)),
            pltpu.SemaphoreType.DMA((2, 30)),
        ],
        compiler_params=pltpu.CompilerParams(
            collective_id=0, has_side_effects=True, vmem_limit_bytes=60 * 1024 * 1024
        ),
        name="distill",
    )(
        teacher_rows,
        student_rows,
        teacher_gain,
        student_gain,
        teacher_head,
        student_head,
        route,
        target.reshape(1, all_rows),
    )
    return (loss.reshape(all_rows), grad)


def solution(mesh):
    placed = (
        P(("group", "vocab"), None),
        P(("group", "vocab"), None),
        P(),
        P(),
        P(None, "vocab"),
        P(None, "vocab"),
        P(),
        P("group"),
    )
    return jax.shard_map(
        local,
        mesh=mesh,
        in_specs=placed,
        out_specs=(P("group"), P(("group", "vocab"), None)),
        check_vma=False,
    )
```

```python
import functools

import jax
import jax.numpy as jnp
from jax import lax
from jax.experimental import pallas as pl
from jax.experimental.pallas import tpu as pltpu
from jax.sharding import PartitionSpec as P

MESH = pl.DeviceIdType.MESH
epsilon = 1e-06
loss_scale = 16.0
distill_mix = 0.5

RING = 4
CORES = 2
BLOCKS = RING * RING
SUB = 16
STEPS = (0, -1, 1, 2)
GATHER_COPIES = 6 + 6 * RING


def contract_last(left_side, right_side):
    return lax.dot_general(
        left_side, right_side, (((1,), (1,)), ((), ())), preferred_element_type=jnp.float32
    )


class Place:
    def __init__(self):
        self.group = lax.axis_index("group")
        self.vocab = lax.axis_index("vocab")
        self.core = lax.rem(self.vocab, CORES)
        self.zh = lax.rem(self.vocab // CORES, RING)
        self.x = self.vocab // (CORES * RING)

    def block(self, dx, dz):
        xx, zz = lax.rem(self.x + dx + RING, RING), lax.rem(self.zh + dz + RING, RING)
        return xx * RING + zz

    def dev(self, dx, dz):
        return (self.group, self.block(dx, dz) * CORES + self.core)

    def nth(self, d):
        return (self.group, lax.rem(self.block(0, 0) + d, BLOCKS) * CORES + self.core)

    def other(self):
        return (self.group, self.block(0, 0) * CORES + 1 - self.core)


class Gather:
    def __init__(self, buf, sem, place, sends):
        self.buf, self.sem, self.place, self.sends = buf, sem, place, sends
        self.width = buf.shape[2] // 2

    def copy(self, index, dx, dz, h, dev):
        view = self.buf.at[self.place.block(dx, dz), :, pl.ds(h * self.width, self.width)]
        return pltpu.make_async_remote_copy(
            src_ref=view,
            dst_ref=view,
            send_sem=self.sem.at[0, index],
            recv_sem=self.sem.at[1, index],
            device_id=dev,
            device_id_type=MESH,
        )

    def go(self, *args):
        copy = self.copy(*args)
        copy.start()
        self.sends.append(copy)

    def wait(self, index, dx, dz, h):
        self.copy(index, dx, dz, h, self.place.dev(1, 0)).wait_recv()

    def start(self):
        up, down = self.place.dev(0, 1), self.place.dev(0, -1)
        self.go(0, 0, 0, 0, up)
        self.go(2, 0, 0, 1, down)
        self.go(1, 0, 0, 1, up)
        self.go(3, 0, 0, 0, down)
        self.x_half(0, 0)
        self.x_half(0, 1)

    def x_half(self, j, h):
        up, down = self.place.dev(1, 0), self.place.dev(-1, 0)
        base, dz = 6 + 6 * j, STEPS[j]
        if h == 0:
            self.go(base, 0, dz, 0, up)
            self.go(base + 3, 0, dz, 0, down)
        else:
            self.go(base + 2, 0, dz, 1, down)
            self.go(base + 1, 0, dz, 1, up)

    def z_forward(self):
        self.wait(0, 0, -1, 0)
        self.go(4, 0, -1, 0, self.place.dev(0, 1))
        self.x_half(1, 0)
        self.wait(2, 0, 1, 1)
        self.go(5, 0, 1, 1, self.place.dev(0, -1))
        self.x_half(2, 1)

    def z_near(self):
        self.wait(1, 0, -1, 1)
        self.x_half(1, 1)
        self.wait(3, 0, 1, 0)
        self.x_half(2, 0)

    def z_far(self, direct):
        up, down, opposite = self.place.dev(1, 0), self.place.dev(-1, 0), self.place.dev(2, 0)
        base = 6 + 6 * 3
        self.wait(4, 0, 2, 0)
        if direct:
            self.go(base + 4, 0, 2, 0, opposite)
        self.go(base, 0, 2, 0, up)
        self.go(base + 3, 0, 2, 0, down)
        self.wait(5, 0, 2, 1)
        if direct:
            self.go(base + 5, 0, 2, 1, opposite)
        self.go(base + 2, 0, 2, 1, down)
        self.go(base + 1, 0, 2, 1, up)

    def x_forward(self, j):
        base, dz = 6 + 6 * j, STEPS[j]
        self.wait(base, -1, dz, 0)
        self.go(base + 4, -1, dz, 0, self.place.dev(1, 0))
        self.wait(base + 2, 1, dz, 1)
        self.go(base + 5, 1, dz, 1, self.place.dev(-1, 0))

    def x_done(self, j, direct=False):
        base, dz = 6 + 6 * j, STEPS[j]
        if direct:
            self.wait(base, -1, dz, 0)
            self.wait(base + 2, 1, dz, 1)
        self.wait(base + 1, -1, dz, 1)
        self.wait(base + 3, 1, dz, 0)
        self.wait(base + 4, 2, dz, 0)
        self.wait(base + 5, 2, dz, 1)


def kernel(
    groups,
    teacher_rows_in,
    student_rows_in,
    teacher_gain_in,
    student_gain_in,
    teacher_head,
    student_head,
    route_in,
    target_in,
    loss_out,
    grad_out,
    teacher_rows,
    student_rows,
    teacher_gain,
    student_gain,
    route,
    target,
    head_t,
    head_s,
    rows_t,
    rows_s,
    wide,
    out_rows,
    in_rows,
    routed,
    hat_keep,
    inverse_keep,
    target_keep,
    logits_t,
    logits_s,
    exp_s,
    stat_all,
    columns_keep,
    part,
    xf_out,
    xf_in,
    xn_out,
    xn_in,
    z_part,
    zf_out,
    zf_in,
    zn_out,
    zn_in,
    local_sem,
    head_sem,
    route_sem,
    gather_t_sem,
    gather_s_sem,
    stat_sem,
    back_sem,
):
    p = Place()
    g, v, core = p.group, p.vocab, p.core
    f32, bf16 = jnp.float32, jnp.bfloat16
    local_rows, dt = teacher_rows.shape
    ds = student_rows.shape[1]
    shard = head_s.shape[2]
    ht, hs = dt // 2, ds // 2
    qs = hs // 2
    rows = BLOCKS * local_rows
    chunk = dt // SUB
    sends = []

    def remote(src, dst, sem, index, dev):
        copy = pltpu.make_async_remote_copy(
            src_ref=src,
            dst_ref=dst,
            send_sem=sem.at[0, index],
            recv_sem=sem.at[1, index],
            device_id=dev,
            device_id_type=MESH,
        )
        copy.start()
        sends.append(copy)
        return copy

    def fetch(src, dst, index):
        copy = pltpu.make_async_copy(src, dst, local_sem.at[index])
        copy.start()
        return copy

    barrier = pltpu.get_barrier_semaphore()

    def greet(dev):
        pl.semaphore_signal(barrier, inc=1, device_id=dev, device_id_type=MESH)

    load_rows_s = fetch(student_rows_in, student_rows, 0)
    load_gain_s = fetch(student_gain_in, student_gain, 1)
    load_rows_t = fetch(teacher_rows_in, teacher_rows, 2)
    load_gain_t = fetch(teacher_gain_in, teacher_gain, 3)
    load_route = fetch(route_in, route, 4)
    load_target = fetch(target_in, target, 5)
    load_head_s = fetch(student_head, head_s.at[core], 6)
    load_head_t = fetch(teacher_head, head_t.at[core], 7)
    for d in range(1, RING):
        greet(p.dev(d, 0))
    greet(p.dev(0, 1))
    greet(p.dev(0, -1))
    greet(p.other())
    for d in range(1, groups):
        greet((lax.rem(g + d, groups), v))

    load_rows_s.wait()
    load_gain_s.wait()
    here = p.block(0, 0)
    wide_s = student_rows[...].astype(f32)
    inverse = lax.rsqrt(jnp.mean(wide_s * wide_s, axis=1, keepdims=True) + epsilon)
    inverse_keep[...] = jnp.broadcast_to(inverse, inverse_keep.shape)
    hat = wide_s * inverse
    hat_keep[...] = hat
    gain_s = student_gain[...].astype(f32).reshape(1, ds)
    normed_s = hat * gain_s
    rows_s[here] = jnp.concatenate([normed_s[:, :hs], normed_s[:, hs:]], axis=0).astype(bf16)

    load_rows_t.wait()
    load_gain_t.wait()
    load_route.wait()
    wide_t = teacher_rows[...].astype(f32)
    inverse_t = lax.rsqrt(jnp.mean(wide_t * wide_t, axis=1, keepdims=True) + epsilon)
    normed_t = wide_t * inverse_t * teacher_gain[...].astype(f32).reshape(1, dt)
    for c in range(SUB):
        wide[:, c, :] = normed_t[:, c * chunk : (c + 1) * chunk]
    span = lax.axis_size("vocab") * local_rows
    first = g * span + v * local_rows
    my_routes = [route[first + k] for k in range(local_rows)]

    @pl.loop(0, groups)
    def _(dest):
        total = jnp.zeros((SUB, chunk), f32)
        for k in range(local_rows):
            total += jnp.where(my_routes[k] == dest, 1.0, 0.0) * wide[k]
        out_rows[dest] = total.astype(bf16)

    in_rows[g] = out_rows[g]
    pl.semaphore_wait(barrier, groups - 1 + RING - 1 + 2 + 1)

    student = Gather(rows_s, gather_s_sem, p, sends)
    teacher = Gather(rows_t, gather_t_sem, p, sends)
    student.start()

    routed_copies = []
    for d in range(1, groups):
        dest = lax.rem(g + d, groups)
        routed_copies.append(
            remote(out_rows.at[dest], in_rows.at[g], route_sem, d, (dest, v))
        )
    fetch_head_s = remote(student_head, head_s.at[core], head_sem, 0, p.other())
    fetch_head_t = remote(teacher_head, head_t.at[core], head_sem, 1, p.other())

    student.x_forward(0)
    student.z_forward()
    student.z_near()

    ranks, valids = [], []
    seen = jnp.int32(0)
    for t in range(groups):
        start = t * span + v * local_rows
        valid = jnp.int32(0)
        for k in range(local_rows):
            valid += jnp.where(route[start + k] == g, 1, 0)
        ranks.append(seen)
        valids.append(valid)
        seen = seen + valid
    for copy in routed_copies:
        copy.wait_recv()
    for j in range(local_rows):
        total = jnp.zeros((SUB, chunk), f32)
        for t in range(groups):
            weight = jnp.where(ranks[t] == j, valids[t], 0).astype(f32)
            total += weight * in_rows[t].astype(f32)
        wide[j] = total
    for c in range(SUB):
        half, at = divmod(c * chunk, ht)
        routed[half * 8 : half * 8 + 8, at : at + chunk] = wide[:, c, :]
    rows_t[here] = routed[...].astype(bf16)
    teacher.start()

    teacher.x_forward(0)
    student.z_far(False)
    student.x_forward(1)
    student.x_forward(2)
    teacher.z_forward()
    teacher.z_near()
    student.x_forward(3)

    load_target.wait()
    all_targets = jnp.transpose(jnp.broadcast_to(target[...].astype(f32), (128, 2 * rows)))
    target_keep[...] = all_targets
    columns = (v // CORES) * (CORES * shard) + lax.broadcasted_iota(
        jnp.int32, (rows, CORES * shard), 1
    )
    my_targets = jnp.concatenate(
        [
            target_keep[pl.ds(pl.multiple_of(b * 16 + core * 8, 8), 8), :]
            for b in range(BLOCKS)
        ],
        axis=0,
    )[:, 0:1].astype(jnp.int32)

    def logits(left, count, head, half):
        parts = []
        for c in range(CORES):
            low = jnp.dot(left, head[c, 0:half, :], preferred_element_type=f32)
            high = jnp.dot(left, head[c, half : 2 * half, :], preferred_element_type=f32)
            low = low.reshape(count, 16, shard)[:, 0:8]
            high = high.reshape(count, 16, shard)[:, 8:16]
            parts.append((low + high).reshape(count * 8, shard))
        return jnp.concatenate(parts, axis=1)

    teacher.x_forward(1)
    teacher.x_forward(2)
    teacher.z_far(True)
    for j in range(RING):
        student.x_done(j)
    load_head_s.wait()
    fetch_head_s.wait_recv()
    values = logits(rows_s[...].reshape(BLOCKS * 16, hs), BLOCKS, head_s, hs)
    logits_s[...] = values
    top_s = jnp.max(values, axis=1, keepdims=True)
    powers = jnp.exp(values - top_s)
    exp_s[...] = powers
    sum_s = jnp.sum(powers, axis=1, keepdims=True)
    picked = jnp.sum(jnp.where(columns == my_targets, values, 0.0), axis=1, keepdims=True)


    def teacher_logits(steps):
        blocks = [p.block(dx, STEPS[j]) for j in steps for dx in range(RING)]
        left = jnp.concatenate([rows_t[b] for b in blocks], axis=0)
        values = logits(left, len(blocks), head_t, ht)
        for i, b in enumerate(blocks):
            logits_t[pl.ds(pl.multiple_of(b * 8, 8), 8), :] = values[i * 8 : i * 8 + 8]

    load_head_t.wait()
    fetch_head_t.wait_recv()
    for j in range(3):
        teacher.x_done(j)
    teacher_logits((0, 1, 2))
    teacher.x_done(3, True)
    teacher_logits((3,))

    values = logits_t[...]
    top_t = jnp.max(values, axis=1, keepdims=True)
    exp_t = jnp.exp(values - top_t)
    sum_t = jnp.sum(exp_t, axis=1, keepdims=True)
    cross = jnp.sum(exp_t * (values - logits_s[...]), axis=1, keepdims=True)

    lane = lax.broadcasted_iota(jnp.int32, (rows, 128), 1)
    packed = jnp.zeros((rows, 128), f32)
    for i, value in enumerate((top_t, top_s, top_t, None, sum_t, sum_s, cross, picked)):
        if value is not None:
            packed = jnp.where(lane == i, value, packed)
    stats = jnp.transpose(packed)[0:8, :]

    stat_all[here] = stats
    copies = [
        remote(stat_all.at[here], stat_all.at[here], stat_sem, d, p.nth(d))
        for d in range(1, BLOCKS)
    ]
    for copy in copies:
        copy.wait_recv()
    parts = [stat_all[i] for i in range(BLOCKS)]
    tops = functools.reduce(jnp.maximum, [part[0:4] for part in parts])
    sums = sum(jnp.exp(part[0:4] - tops) * part[4:8] for part in parts)
    merged = jnp.concatenate([tops, sums], axis=0)
    all_top_t, all_top_s = merged[0:1], merged[1:2]
    all_sum_t, all_sum_s = merged[4:5], merged[5:6]
    scale_t = (loss_scale * distill_mix) * jnp.exp(stats[0:1] - all_top_t) / all_sum_t
    scale_s = loss_scale * jnp.exp(stats[1:2] - all_top_s) / all_sum_s
    lse_t = all_top_t + jnp.log(all_sum_t)
    lse_s = all_top_s + jnp.log(all_sum_s)
    loss = distill_mix * (merged[6:7] / all_sum_t - lse_t + lse_s) + (1.0 - distill_mix) * (
        lse_s - merged[7:8]
    )
    turned = jnp.transpose(
        jnp.concatenate([scale_t, scale_s, loss, jnp.zeros((125, rows), f32)], axis=0)
    )
    columns_keep[core] = turned
    loss_copy = remote(columns_keep.at[core], columns_keep.at[core], head_sem, 2, p.other())
    logit_grad = (
        exp_s[...] * turned[:, 1:2]
        - exp_t * turned[:, 0:1]
        - jnp.where(columns == my_targets, loss_scale * (1.0 - distill_mix), 0.0)
    ).astype(bf16)

    step = qs // 2
    for n in range(ds // step):
        half, at = divmod(n * step, hs)
        block = contract_last(
            logit_grad[:, 0:shard], head_s[0, n * step : (n + 1) * step, :]
        ) + contract_last(logit_grad[:, shard:], head_s[1, n * step : (n + 1) * step, :])
        part[:, half * 8 : half * 8 + 8, at : at + step] = block.reshape(
            BLOCKS, local_rows, step
        )

    order = (2, 1, -1, 0)
    plus_x, minus_x = p.dev(1, 0), p.dev(-1, 0)
    plus_z, minus_z = p.dev(0, 1), p.dev(0, -1)
    cols = (slice(0, qs), slice(qs, hs))
    far_copies, near_copies = {}, {}

    def x_first(i):
        far, up, down = (part.at[p.block(d, order[i])] for d in (2, 1, -1))
        xf_out[i, 0] = far[:, cols[0]].astype(bf16)
        xf_out[i, 1] = far[:, cols[1]].astype(bf16)
        far_copies[i] = (
            remote(xf_out.at[i, 0], xf_in.at[i, 0], back_sem, 2 * i, plus_x),
            remote(xf_out.at[i, 1], xf_in.at[i, 1], back_sem, 1 + 2 * i, minus_x),
        )
        xn_out[i, 0, 1] = up[:, cols[1]].astype(bf16)
        xn_out[i, 1, 0] = down[:, cols[0]].astype(bf16)
        near_copies[i] = [
            remote(xn_out.at[i, 0, 1], xn_in.at[i, 0, 1], back_sem, 8 + 2 * i, plus_x),
            remote(xn_out.at[i, 1, 0], xn_in.at[i, 1, 0], back_sem, 9 + 2 * i, minus_x),
        ]

    def x_whole(i):
        slots = (xf_out.at[i], xn_out.at[i, 0], xn_out.at[i, 1])
        for slot, d in zip(slots, (2, 1, -1)):
            block = part.at[p.block(d, order[i])]
            for h in range(2):
                slot[h] = block[:, cols[h]].astype(bf16)
        near_copies[i] = [
            remote(slots[0], xf_in.at[i], back_sem, 2 * i, p.dev(2, 0)),
            remote(slots[1], xn_in.at[i, 0], back_sem, 8 + 2 * i, plus_x),
            remote(slots[2], xn_in.at[i, 1], back_sem, 9 + 2 * i, minus_x),
        ]

    def x_second(i):
        up, down = (part.at[p.block(d, order[i])] for d in (1, -1))
        far_copies[i][0].wait_recv()
        xn_out[i, 0, 0] = (up[:, cols[0]] + xf_in[i, 0].astype(f32)).astype(bf16)
        near_copies[i].append(
            remote(xn_out.at[i, 0, 0], xn_in.at[i, 0, 0], back_sem, 16 + 2 * i, plus_x)
        )
        far_copies[i][1].wait_recv()
        xn_out[i, 1, 1] = (down[:, cols[1]] + xf_in[i, 1].astype(f32)).astype(bf16)
        near_copies[i].append(
            remote(xn_out.at[i, 1, 1], xn_in.at[i, 1, 1], back_sem, 17 + 2 * i, minus_x)
        )

    def x_done(i):
        for copy in near_copies[i]:
            copy.wait_recv()
        block = part.at[p.block(0, order[i])]
        return [
            block[:, cols[h]] + xn_in[i, 0, h].astype(f32) + xn_in[i, 1, h].astype(f32)
            for h in range(2)
        ]

    x_whole(0)
    x_first(1)
    x_first(2)
    x_first(3)
    x_second(1)
    x_second(2)
    z_far = []
    for h, value in enumerate(x_done(0)):
        zf_out[h] = (value + xf_in[0, h].astype(f32)).astype(bf16)
        z_far.append(
            remote(zf_out.at[h], zf_in.at[h], back_sem, 24 + h, (plus_z, minus_z)[h])
        )
    x_second(3)
    up = x_done(1)
    zn_out[0, 1] = up[1].astype(bf16)
    z_near = [remote(zn_out.at[0, 1], zn_in.at[0, 1], back_sem, 26, plus_z)]
    z_part[0] = up[0]
    down = x_done(2)
    zn_out[1, 0] = down[0].astype(bf16)
    z_near.append(remote(zn_out.at[1, 0], zn_in.at[1, 0], back_sem, 27, minus_z))
    z_part[1] = down[1]
    z_far[0].wait_recv()
    zn_out[0, 0] = (z_part[0] + zf_in[0].astype(f32)).astype(bf16)
    z_near.append(remote(zn_out.at[0, 0], zn_in.at[0, 0], back_sem, 28, plus_z))
    z_far[1].wait_recv()
    zn_out[1, 1] = (z_part[1] + zf_in[1].astype(f32)).astype(bf16)
    z_near.append(remote(zn_out.at[1, 1], zn_in.at[1, 1], back_sem, 29, minus_z))
    for h, value in enumerate(x_done(3)):
        z_part[2 + h] = value

    loss_copy.wait_recv()
    both = jnp.concatenate(
        [columns_keep[c, b * 8 : b * 8 + 8, :] for b in range(BLOCKS) for c in range(CORES)],
        axis=0,
    )
    loss_out[...] = jnp.transpose(both)[2:3, :]
    inverse = inverse_keep[:, 0:1]
    hat = hat_keep[...]
    gain = student_gain[...].astype(f32).reshape(1, ds)

    for copy in z_near:
        copy.wait_recv()
    mine = [
        z_part[2 + h] + zn_in[0, h].astype(f32) + zn_in[1, h].astype(f32) for h in range(2)
    ]
    scaled = (
        jnp.concatenate([mine[0][0:8], mine[1][0:8], mine[0][8:16], mine[1][8:16]], axis=1)
        * gain
    )
    grad_out[...] = (
        inverse * (scaled - hat * jnp.mean(scaled * hat, axis=1, keepdims=True))
    ).astype(bf16)

    for copy in sends:
        copy.wait_send()


def local(
    teacher_rows,
    student_rows,
    teacher_gain,
    student_gain,
    teacher_head,
    student_head,
    route,
    target,
):
    groups = lax.axis_size("group")
    f32, bf16 = jnp.float32, jnp.bfloat16
    local_rows, dt = teacher_rows.shape
    ds = student_rows.shape[1]
    shard = teacher_head.shape[1]
    all_rows = target.shape[0]
    rows = all_rows // CORES
    ht, hs = dt // 2, ds // 2
    qs, chunk = hs // 2, dt // SUB
    vmem = pl.BlockSpec(memory_space=pltpu.VMEM)
    anywhere = pl.BlockSpec(memory_space=pl.ANY)
    loss, grad = pl.pallas_call(
        functools.partial(kernel, groups),
        out_shape=(
            jax.ShapeDtypeStruct((1, all_rows), f32),
            jax.ShapeDtypeStruct((local_rows, ds), bf16),
        ),
        in_specs=[anywhere] * 8,
        out_specs=(vmem, vmem),
        scratch_shapes=[
            pltpu.VMEM((local_rows, dt), bf16),
            pltpu.VMEM((local_rows, ds), bf16),
            pltpu.VMEM((dt,), bf16),
            pltpu.VMEM((ds,), bf16),
            pltpu.SMEM(route.shape, jnp.int32),
            pltpu.VMEM((1, all_rows), jnp.int32),
            pltpu.VMEM((CORES, dt, shard), bf16),
            pltpu.VMEM((CORES, ds, shard), bf16),
            pltpu.VMEM((BLOCKS, 16, ht), bf16),
            pltpu.VMEM((BLOCKS, 16, hs), bf16),
            pltpu.VMEM((local_rows, SUB, chunk), f32),
            pltpu.VMEM((groups, SUB, chunk), bf16),
            pltpu.VMEM((groups, SUB, chunk), bf16),
            pltpu.VMEM((16, ht), f32),
            pltpu.VMEM((local_rows, ds), f32),
            pltpu.VMEM((local_rows, 128), f32),
            pltpu.VMEM((all_rows, 128), f32),
            pltpu.VMEM((rows, CORES * shard), f32),
            pltpu.VMEM((rows, CORES * shard), f32),
            pltpu.VMEM((rows, CORES * shard), f32),
            pltpu.VMEM((BLOCKS, 8, rows), f32),
            pltpu.VMEM((CORES, rows, 128), f32),
            pltpu.VMEM((BLOCKS, 16, hs), f32),
            pltpu.VMEM((4, 2, 16, qs), bf16),
            pltpu.VMEM((4, 2, 16, qs), bf16),
            pltpu.VMEM((4, 2, 2, 16, qs), bf16),
            pltpu.VMEM((4, 2, 2, 16, qs), bf16),
            pltpu.VMEM((4, 16, qs), f32),
            pltpu.VMEM((2, 16, qs), bf16),
            pltpu.VMEM((2, 16, qs), bf16),
            pltpu.VMEM((2, 2, 16, qs), bf16),
            pltpu.VMEM((2, 2, 16, qs), bf16),
            pltpu.SemaphoreType.DMA((8,)),
            pltpu.SemaphoreType.DMA((2, 3)),
            pltpu.SemaphoreType.DMA((2, groups)),
            pltpu.SemaphoreType.DMA((2, GATHER_COPIES)),
            pltpu.SemaphoreType.DMA((2, GATHER_COPIES)),
            pltpu.SemaphoreType.DMA((2, BLOCKS)),
            pltpu.SemaphoreType.DMA((2, 30)),
        ],
        compiler_params=pltpu.CompilerParams(
            collective_id=0, has_side_effects=True, vmem_limit_bytes=60 * 1024 * 1024
        ),
        name="distill",
    )(
        teacher_rows,
        student_rows,
        teacher_gain,
        student_gain,
        teacher_head,
        student_head,
        route,
        target.reshape(1, all_rows),
    )
    return (loss.reshape(all_rows), grad)


def solution(mesh):
    placed = (
        P(("group", "vocab"), None),
        P(("group", "vocab"), None),
        P(),
        P(),
        P(None, "vocab"),
        P(None, "vocab"),
        P(),
        P("group"),
    )
    return jax.shard_map(
        local,
        mesh=mesh,
        in_specs=placed,
        out_specs=(P("group"), P(("group", "vocab"), None)),
        check_vma=False,
    )
```

```python
import functools

import jax
import jax.numpy as jnp
from jax import lax
from jax.experimental import pallas as pl
from jax.experimental.pallas import tpu as pltpu
from jax.sharding import PartitionSpec as P

MESH = pl.DeviceIdType.MESH
epsilon = 1e-06
loss_scale = 16.0
distill_mix = 0.5

RING = 4
CORES = 2
BLOCKS = RING * RING
SUB = 16
STEPS = (0, -1, 1, 2)
GATHER_COPIES = 6 + 6 * RING


def contract_last(left_side, right_side):
    return lax.dot_general(
        left_side, right_side, (((1,), (1,)), ((), ())), preferred_element_type=jnp.float32
    )


class Place:
    def __init__(self):
        self.group = lax.axis_index("group")
        self.vocab = lax.axis_index("vocab")
        self.core = lax.rem(self.vocab, CORES)
        self.zh = lax.rem(self.vocab // CORES, RING)
        self.x = self.vocab // (CORES * RING)

    def block(self, dx, dz):
        xx, zz = lax.rem(self.x + dx + RING, RING), lax.rem(self.zh + dz + RING, RING)
        return xx * RING + zz

    def dev(self, dx, dz):
        return (self.group, self.block(dx, dz) * CORES + self.core)

    def nth(self, d):
        return (self.group, lax.rem(self.block(0, 0) + d, BLOCKS) * CORES + self.core)

    def other(self):
        return (self.group, self.block(0, 0) * CORES + 1 - self.core)


class Gather:
    def __init__(self, buf, sem, place, sends):
        self.buf, self.sem, self.place, self.sends = buf, sem, place, sends
        self.width = buf.shape[2] // 2

    def copy(self, index, dx, dz, h, dev):
        view = self.buf.at[self.place.block(dx, dz), :, pl.ds(h * self.width, self.width)]
        return pltpu.make_async_remote_copy(
            src_ref=view,
            dst_ref=view,
            send_sem=self.sem.at[0, index],
            recv_sem=self.sem.at[1, index],
            device_id=dev,
            device_id_type=MESH,
        )

    def go(self, *args):
        copy = self.copy(*args)
        copy.start()
        self.sends.append(copy)

    def wait(self, index, dx, dz, h):
        self.copy(index, dx, dz, h, self.place.dev(1, 0)).wait_recv()

    def start(self):
        up, down = self.place.dev(0, 1), self.place.dev(0, -1)
        self.go(0, 0, 0, 0, up)
        self.go(2, 0, 0, 1, down)
        self.go(1, 0, 0, 1, up)
        self.go(3, 0, 0, 0, down)
        self.x_half(0, 0)
        self.x_half(0, 1)

    def x_half(self, j, h):
        up, down = self.place.dev(1, 0), self.place.dev(-1, 0)
        base, dz = 6 + 6 * j, STEPS[j]
        if h == 0:
            self.go(base, 0, dz, 0, up)
            self.go(base + 3, 0, dz, 0, down)
        else:
            self.go(base + 2, 0, dz, 1, down)
            self.go(base + 1, 0, dz, 1, up)

    def z_forward(self):
        self.wait(0, 0, -1, 0)
        self.go(4, 0, -1, 0, self.place.dev(0, 1))
        self.x_half(1, 0)
        self.wait(2, 0, 1, 1)
        self.go(5, 0, 1, 1, self.place.dev(0, -1))
        self.x_half(2, 1)

    def z_near(self):
        self.wait(1, 0, -1, 1)
        self.x_half(1, 1)
        self.wait(3, 0, 1, 0)
        self.x_half(2, 0)

    def z_far(self, direct):
        up, down, opposite = self.place.dev(1, 0), self.place.dev(-1, 0), self.place.dev(2, 0)
        base = 6 + 6 * 3
        self.wait(4, 0, 2, 0)
        if direct:
            self.go(base + 4, 0, 2, 0, opposite)
        self.go(base, 0, 2, 0, up)
        self.go(base + 3, 0, 2, 0, down)
        self.wait(5, 0, 2, 1)
        if direct:
            self.go(base + 5, 0, 2, 1, opposite)
        self.go(base + 2, 0, 2, 1, down)
        self.go(base + 1, 0, 2, 1, up)

    def x_forward(self, j):
        base, dz = 6 + 6 * j, STEPS[j]
        self.wait(base, -1, dz, 0)
        self.go(base + 4, -1, dz, 0, self.place.dev(1, 0))
        self.wait(base + 2, 1, dz, 1)
        self.go(base + 5, 1, dz, 1, self.place.dev(-1, 0))

    def x_done(self, j, direct=False):
        base, dz = 6 + 6 * j, STEPS[j]
        if direct:
            self.wait(base, -1, dz, 0)
            self.wait(base + 2, 1, dz, 1)
        self.wait(base + 1, -1, dz, 1)
        self.wait(base + 3, 1, dz, 0)
        self.wait(base + 4, 2, dz, 0)
        self.wait(base + 5, 2, dz, 1)


def kernel(
    groups,
    teacher_rows_in,
    student_rows_in,
    teacher_gain_in,
    student_gain_in,
    teacher_head,
    student_head,
    route_in,
    target_in,
    loss_out,
    grad_out,
    teacher_rows,
    student_rows,
    teacher_gain,
    student_gain,
    route,
    target,
    head_t,
    head_s,
    rows_t,
    rows_s,
    wide,
    out_rows,
    in_rows,
    routed,
    hat_keep,
    inverse_keep,
    target_keep,
    logits_t,
    logits_s,
    exp_s,
    stat_all,
    columns_keep,
    part,
    xf_out,
    xf_in,
    xn_out,
    xn_in,
    z_part,
    zf_out,
    zf_in,
    zn_out,
    zn_in,
    local_sem,
    head_sem,
    route_sem,
    gather_t_sem,
    gather_s_sem,
    stat_sem,
    back_sem,
):
    p = Place()
    g, v, core = p.group, p.vocab, p.core
    f32, bf16 = jnp.float32, jnp.bfloat16
    local_rows, dt = teacher_rows.shape
    ds = student_rows.shape[1]
    shard = head_s.shape[2]
    ht, hs = dt // 2, ds // 2
    qs = hs // 2
    rows = BLOCKS * local_rows
    chunk = dt // SUB
    sends = []

    def remote(src, dst, sem, index, dev):
        copy = pltpu.make_async_remote_copy(
            src_ref=src,
            dst_ref=dst,
            send_sem=sem.at[0, index],
            recv_sem=sem.at[1, index],
            device_id=dev,
            device_id_type=MESH,
        )
        copy.start()
        sends.append(copy)
        return copy

    def fetch(src, dst, index):
        copy = pltpu.make_async_copy(src, dst, local_sem.at[index])
        copy.start()
        return copy

    barrier = pltpu.get_barrier_semaphore()

    def greet(dev):
        pl.semaphore_signal(barrier, inc=1, device_id=dev, device_id_type=MESH)

    load_rows_s = fetch(student_rows_in, student_rows, 0)
    load_gain_s = fetch(student_gain_in, student_gain, 1)
    load_rows_t = fetch(teacher_rows_in, teacher_rows, 2)
    load_gain_t = fetch(teacher_gain_in, teacher_gain, 3)
    load_route = fetch(route_in, route, 4)
    load_target = fetch(target_in, target, 5)
    load_head_s = fetch(student_head, head_s.at[core], 6)
    load_head_t = fetch(teacher_head, head_t.at[core], 7)
    for d in range(1, RING):
        greet(p.dev(d, 0))
    greet(p.dev(0, 1))
    greet(p.dev(0, -1))
    greet(p.other())
    for d in range(1, groups):
        greet((lax.rem(g + d, groups), v))

    load_rows_s.wait()
    load_gain_s.wait()
    here = p.block(0, 0)
    wide_s = student_rows[...].astype(f32)
    inverse = lax.rsqrt(jnp.mean(wide_s * wide_s, axis=1, keepdims=True) + epsilon)
    inverse_keep[...] = jnp.broadcast_to(inverse, inverse_keep.shape)
    hat = wide_s * inverse
    hat_keep[...] = hat
    gain_s = student_gain[...].astype(f32).reshape(1, ds)
    normed_s = hat * gain_s
    rows_s[here] = jnp.concatenate([normed_s[:, :hs], normed_s[:, hs:]], axis=0).astype(bf16)

    load_rows_t.wait()
    load_gain_t.wait()
    load_route.wait()
    wide_t = teacher_rows[...].astype(f32)
    inverse_t = lax.rsqrt(jnp.mean(wide_t * wide_t, axis=1, keepdims=True) + epsilon)
    normed_t = wide_t * inverse_t * teacher_gain[...].astype(f32).reshape(1, dt)
    for c in range(SUB):
        wide[:, c, :] = normed_t[:, c * chunk : (c + 1) * chunk]
    span = lax.axis_size("vocab") * local_rows
    first = g * span + v * local_rows
    my_routes = [route[first + k] for k in range(local_rows)]

    @pl.loop(0, groups)
    def _(dest):
        total = jnp.zeros((SUB, chunk), f32)
        for k in range(local_rows):
            total += jnp.where(my_routes[k] == dest, 1.0, 0.0) * wide[k]
        out_rows[dest] = total.astype(bf16)

    in_rows[g] = out_rows[g]
    pl.semaphore_wait(barrier, groups - 1 + RING - 1 + 2 + 1)

    student = Gather(rows_s, gather_s_sem, p, sends)
    teacher = Gather(rows_t, gather_t_sem, p, sends)
    student.start()

    routed_copies = []
    for d in range(1, groups):
        dest = lax.rem(g + d, groups)
        routed_copies.append(
            remote(out_rows.at[dest], in_rows.at[g], route_sem, d, (dest, v))
        )
    fetch_head_s = remote(student_head, head_s.at[core], head_sem, 0, p.other())
    fetch_head_t = remote(teacher_head, head_t.at[core], head_sem, 1, p.other())

    student.x_forward(0)
    student.z_forward()
    student.z_near()

    ranks, valids = [], []
    seen = jnp.int32(0)
    for t in range(groups):
        start = t * span + v * local_rows
        valid = jnp.int32(0)
        for k in range(local_rows):
            valid += jnp.where(route[start + k] == g, 1, 0)
        ranks.append(seen)
        valids.append(valid)
        seen = seen + valid
    for copy in routed_copies:
        copy.wait_recv()
    for j in range(local_rows):
        total = jnp.zeros((SUB, chunk), f32)
        for t in range(groups):
            weight = jnp.where(ranks[t] == j, valids[t], 0).astype(f32)
            total += weight * in_rows[t].astype(f32)
        wide[j] = total
    for c in range(SUB):
        half, at = divmod(c * chunk, ht)
        routed[half * 8 : half * 8 + 8, at : at + chunk] = wide[:, c, :]
    rows_t[here] = routed[...].astype(bf16)
    teacher.start()

    teacher.x_forward(0)
    student.z_far(False)
    student.x_forward(1)
    student.x_forward(2)
    teacher.z_forward()
    teacher.z_near()
    student.x_forward(3)

    load_target.wait()
    all_targets = jnp.transpose(jnp.broadcast_to(target[...].astype(f32), (128, 2 * rows)))
    target_keep[...] = all_targets
    columns = (v // CORES) * (CORES * shard) + lax.broadcasted_iota(
        jnp.int32, (rows, CORES * shard), 1
    )
    my_targets = jnp.concatenate(
        [
            target_keep[pl.ds(pl.multiple_of(b * 16 + core * 8, 8), 8), :]
            for b in range(BLOCKS)
        ],
        axis=0,
    )[:, 0:1].astype(jnp.int32)

    def logits(left, count, head, half):
        parts = []
        for c in range(CORES):
            low = jnp.dot(left, head[c, 0:half, :], preferred_element_type=f32)
            high = jnp.dot(left, head[c, half : 2 * half, :], preferred_element_type=f32)
            low = low.reshape(count, 16, shard)[:, 0:8]
            high = high.reshape(count, 16, shard)[:, 8:16]
            parts.append((low + high).reshape(count * 8, shard))
        return jnp.concatenate(parts, axis=1)

    teacher.x_forward(1)
    teacher.x_forward(2)
    teacher.z_far(True)
    for j in range(RING):
        student.x_done(j)
    load_head_s.wait()
    fetch_head_s.wait_recv()
    values = logits(rows_s[...].reshape(BLOCKS * 16, hs), BLOCKS, head_s, hs)
    logits_s[...] = values
    top_s = jnp.max(values, axis=1, keepdims=True)
    powers = jnp.exp(values - top_s)
    exp_s[...] = powers
    sum_s = jnp.sum(powers, axis=1, keepdims=True)
    picked = jnp.sum(jnp.where(columns == my_targets, values, 0.0), axis=1, keepdims=True)


    def teacher_logits(steps):
        blocks = [p.block(dx, STEPS[j]) for j in steps for dx in range(RING)]
        left = jnp.concatenate([rows_t[b] for b in blocks], axis=0)
        values = logits(left, len(blocks), head_t, ht)
        for i, b in enumerate(blocks):
            logits_t[pl.ds(pl.multiple_of(b * 8, 8), 8), :] = values[i * 8 : i * 8 + 8]

    load_head_t.wait()
    fetch_head_t.wait_recv()
    for j in range(3):
        teacher.x_done(j)
    teacher_logits((0, 1, 2))
    teacher.x_done(3, True)
    teacher_logits((3,))

    values = logits_t[...]
    top_t = jnp.max(values, axis=1, keepdims=True)
    exp_t = jnp.exp(values - top_t)
    sum_t = jnp.sum(exp_t, axis=1, keepdims=True)
    cross = jnp.sum(exp_t * (values - logits_s[...]), axis=1, keepdims=True)

    lane = lax.broadcasted_iota(jnp.int32, (rows, 128), 1)
    packed = jnp.zeros((rows, 128), f32)
    for i, value in enumerate((top_t, top_s, top_t, None, sum_t, sum_s, cross, picked)):
        if value is not None:
            packed = jnp.where(lane == i, value, packed)
    stats = jnp.transpose(packed)[0:8, :]

    stat_all[here] = stats
    copies = [
        remote(stat_all.at[here], stat_all.at[here], stat_sem, d, p.nth(d))
        for d in range(1, BLOCKS)
    ]
    for copy in copies:
        copy.wait_recv()
    parts = [stat_all[i] for i in range(BLOCKS)]
    tops = functools.reduce(jnp.maximum, [part[0:4] for part in parts])
    sums = sum(jnp.exp(part[0:4] - tops) * part[4:8] for part in parts)
    merged = jnp.concatenate([tops, sums], axis=0)
    all_top_t, all_top_s = merged[0:1], merged[1:2]
    all_sum_t, all_sum_s = merged[4:5], merged[5:6]
    scale_t = (loss_scale * distill_mix) * jnp.exp(stats[0:1] - all_top_t) / all_sum_t
    scale_s = loss_scale * jnp.exp(stats[1:2] - all_top_s) / all_sum_s
    lse_t = all_top_t + jnp.log(all_sum_t)
    lse_s = all_top_s + jnp.log(all_sum_s)
    loss = distill_mix * (merged[6:7] / all_sum_t - lse_t + lse_s) + (1.0 - distill_mix) * (
        lse_s - merged[7:8]
    )
    turned = jnp.transpose(
        jnp.concatenate([scale_t, scale_s, loss, jnp.zeros((125, rows), f32)], axis=0)
    )
    columns_keep[core] = turned
    loss_copy = remote(columns_keep.at[core], columns_keep.at[core], head_sem, 2, p.other())
    logit_grad = (
        exp_s[...] * turned[:, 1:2]
        - exp_t * turned[:, 0:1]
        - jnp.where(columns == my_targets, loss_scale * (1.0 - distill_mix), 0.0)
    ).astype(bf16)

    order = (2, 1, -1, 0)
    plus_x, minus_x = p.dev(1, 0), p.dev(-1, 0)
    plus_z, minus_z = p.dev(0, 1), p.dev(0, -1)
    cols = (slice(0, qs), slice(qs, hs))
    far_copies, near_copies = {}, {}

    def x_first(i):
        far, up, down = (part.at[p.block(d, order[i])] for d in (2, 1, -1))
        xf_out[i, 0] = far[:, cols[0]].astype(bf16)
        xf_out[i, 1] = far[:, cols[1]].astype(bf16)
        far_copies[i] = (
            remote(xf_out.at[i, 0], xf_in.at[i, 0], back_sem, 2 * i, plus_x),
            remote(xf_out.at[i, 1], xf_in.at[i, 1], back_sem, 1 + 2 * i, minus_x),
        )
        xn_out[i, 0, 1] = up[:, cols[1]].astype(bf16)
        xn_out[i, 1, 0] = down[:, cols[0]].astype(bf16)
        near_copies[i] = [
            remote(xn_out.at[i, 0, 1], xn_in.at[i, 0, 1], back_sem, 8 + 2 * i, plus_x),
            remote(xn_out.at[i, 1, 0], xn_in.at[i, 1, 0], back_sem, 9 + 2 * i, minus_x),
        ]

    def x_whole(i, h):
        slots = (xf_out.at[i, h], xn_out.at[i, 0, h], xn_out.at[i, 1, h])
        for slot, d in zip(slots, (2, 1, -1)):
            slot[...] = part[p.block(d, order[i]), :, cols[h]].astype(bf16)
        return (
            remote(slots[0], xf_in.at[i, h], back_sem, 2 * i + h, p.dev(2, 0)),
            remote(slots[1], xn_in.at[i, 0, h], back_sem, 16 - 8 * h + 2 * i, plus_x),
            remote(slots[2], xn_in.at[i, 1, h], back_sem, 9 + 8 * h + 2 * i, minus_x),
        )

    def x_second(i):
        up, down = (part.at[p.block(d, order[i])] for d in (1, -1))
        far_copies[i][0].wait_recv()
        xn_out[i, 0, 0] = (up[:, cols[0]] + xf_in[i, 0].astype(f32)).astype(bf16)
        near_copies[i].append(
            remote(xn_out.at[i, 0, 0], xn_in.at[i, 0, 0], back_sem, 16 + 2 * i, plus_x)
        )
        far_copies[i][1].wait_recv()
        xn_out[i, 1, 1] = (down[:, cols[1]] + xf_in[i, 1].astype(f32)).astype(bf16)
        near_copies[i].append(
            remote(xn_out.at[i, 1, 1], xn_in.at[i, 1, 1], back_sem, 17 + 2 * i, minus_x)
        )

    def x_done(i):
        for copy in near_copies[i]:
            copy.wait_recv()
        block = part.at[p.block(0, order[i])]
        return [
            block[:, cols[h]] + xn_in[i, 0, h].astype(f32) + xn_in[i, 1, h].astype(f32)
            for h in range(2)
        ]

    step = qs // 2
    whole_copies = []
    for h in range(2):
        for n in (2 * h, 2 * h + 1, 2 * h + 4, 2 * h + 5):
            half, at = divmod(n * step, hs)
            block = contract_last(
                logit_grad[:, 0:shard], head_s[0, n * step : (n + 1) * step, :]
            ) + contract_last(logit_grad[:, shard:], head_s[1, n * step : (n + 1) * step, :])
            part[:, half * 8 : half * 8 + 8, at : at + step] = block.reshape(
                BLOCKS, local_rows, step
            )
        whole_copies.append(x_whole(0, h))
    x_first(1)
    x_first(2)
    x_first(3)
    x_second(1)
    x_second(2)
    z_far = []
    for h in range(2):
        for copy in whole_copies[h]:
            copy.wait_recv()
        zf_out[h] = (
            part[p.block(0, order[0]), :, cols[h]]
            + xf_in[0, h].astype(f32)
            + xn_in[0, 0, h].astype(f32)
            + xn_in[0, 1, h].astype(f32)
        ).astype(bf16)
        z_far.append(
            remote(zf_out.at[h], zf_in.at[h], back_sem, 24 + h, (plus_z, minus_z)[h])
        )
    x_second(3)
    up = x_done(1)
    zn_out[0, 1] = up[1].astype(bf16)
    z_near = [remote(zn_out.at[0, 1], zn_in.at[0, 1], back_sem, 26, plus_z)]
    z_part[0] = up[0]
    down = x_done(2)
    zn_out[1, 0] = down[0].astype(bf16)
    z_near.append(remote(zn_out.at[1, 0], zn_in.at[1, 0], back_sem, 27, minus_z))
    z_part[1] = down[1]
    z_far[0].wait_recv()
    zn_out[0, 0] = (z_part[0] + zf_in[0].astype(f32)).astype(bf16)
    z_near.append(remote(zn_out.at[0, 0], zn_in.at[0, 0], back_sem, 28, plus_z))
    z_far[1].wait_recv()
    zn_out[1, 1] = (z_part[1] + zf_in[1].astype(f32)).astype(bf16)
    z_near.append(remote(zn_out.at[1, 1], zn_in.at[1, 1], back_sem, 29, minus_z))
    for h, value in enumerate(x_done(3)):
        z_part[2 + h] = value

    loss_copy.wait_recv()
    both = jnp.concatenate(
        [columns_keep[c, b * 8 : b * 8 + 8, :] for b in range(BLOCKS) for c in range(CORES)],
        axis=0,
    )
    loss_out[...] = jnp.transpose(both)[2:3, :]
    inverse = inverse_keep[:, 0:1]
    hat = hat_keep[...]
    gain = student_gain[...].astype(f32).reshape(1, ds)

    for copy in z_near:
        copy.wait_recv()
    mine = [
        z_part[2 + h] + zn_in[0, h].astype(f32) + zn_in[1, h].astype(f32) for h in range(2)
    ]
    scaled = (
        jnp.concatenate([mine[0][0:8], mine[1][0:8], mine[0][8:16], mine[1][8:16]], axis=1)
        * gain
    )
    grad_out[...] = (
        inverse * (scaled - hat * jnp.mean(scaled * hat, axis=1, keepdims=True))
    ).astype(bf16)

    for copy in sends:
        copy.wait_send()


def local(
    teacher_rows,
    student_rows,
    teacher_gain,
    student_gain,
    teacher_head,
    student_head,
    route,
    target,
):
    groups = lax.axis_size("group")
    f32, bf16 = jnp.float32, jnp.bfloat16
    local_rows, dt = teacher_rows.shape
    ds = student_rows.shape[1]
    shard = teacher_head.shape[1]
    all_rows = target.shape[0]
    rows = all_rows // CORES
    ht, hs = dt // 2, ds // 2
    qs, chunk = hs // 2, dt // SUB
    vmem = pl.BlockSpec(memory_space=pltpu.VMEM)
    anywhere = pl.BlockSpec(memory_space=pl.ANY)
    loss, grad = pl.pallas_call(
        functools.partial(kernel, groups),
        out_shape=(
            jax.ShapeDtypeStruct((1, all_rows), f32),
            jax.ShapeDtypeStruct((local_rows, ds), bf16),
        ),
        in_specs=[anywhere] * 8,
        out_specs=(vmem, vmem),
        scratch_shapes=[
            pltpu.VMEM((local_rows, dt), bf16),
            pltpu.VMEM((local_rows, ds), bf16),
            pltpu.VMEM((dt,), bf16),
            pltpu.VMEM((ds,), bf16),
            pltpu.SMEM(route.shape, jnp.int32),
            pltpu.VMEM((1, all_rows), jnp.int32),
            pltpu.VMEM((CORES, dt, shard), bf16),
            pltpu.VMEM((CORES, ds, shard), bf16),
            pltpu.VMEM((BLOCKS, 16, ht), bf16),
            pltpu.VMEM((BLOCKS, 16, hs), bf16),
            pltpu.VMEM((local_rows, SUB, chunk), f32),
            pltpu.VMEM((groups, SUB, chunk), bf16),
            pltpu.VMEM((groups, SUB, chunk), bf16),
            pltpu.VMEM((16, ht), f32),
            pltpu.VMEM((local_rows, ds), f32),
            pltpu.VMEM((local_rows, 128), f32),
            pltpu.VMEM((all_rows, 128), f32),
            pltpu.VMEM((rows, CORES * shard), f32),
            pltpu.VMEM((rows, CORES * shard), f32),
            pltpu.VMEM((rows, CORES * shard), f32),
            pltpu.VMEM((BLOCKS, 8, rows), f32),
            pltpu.VMEM((CORES, rows, 128), f32),
            pltpu.VMEM((BLOCKS, 16, hs), f32),
            pltpu.VMEM((4, 2, 16, qs), bf16),
            pltpu.VMEM((4, 2, 16, qs), bf16),
            pltpu.VMEM((4, 2, 2, 16, qs), bf16),
            pltpu.VMEM((4, 2, 2, 16, qs), bf16),
            pltpu.VMEM((4, 16, qs), f32),
            pltpu.VMEM((2, 16, qs), bf16),
            pltpu.VMEM((2, 16, qs), bf16),
            pltpu.VMEM((2, 2, 16, qs), bf16),
            pltpu.VMEM((2, 2, 16, qs), bf16),
            pltpu.SemaphoreType.DMA((8,)),
            pltpu.SemaphoreType.DMA((2, 3)),
            pltpu.SemaphoreType.DMA((2, groups)),
            pltpu.SemaphoreType.DMA((2, GATHER_COPIES)),
            pltpu.SemaphoreType.DMA((2, GATHER_COPIES)),
            pltpu.SemaphoreType.DMA((2, BLOCKS)),
            pltpu.SemaphoreType.DMA((2, 30)),
        ],
        compiler_params=pltpu.CompilerParams(
            collective_id=0, has_side_effects=True, vmem_limit_bytes=60 * 1024 * 1024
        ),
        name="distill",
    )(
        teacher_rows,
        student_rows,
        teacher_gain,
        student_gain,
        teacher_head,
        student_head,
        route,
        target.reshape(1, all_rows),
    )
    return (loss.reshape(all_rows), grad)


def solution(mesh):
    placed = (
        P(("group", "vocab"), None),
        P(("group", "vocab"), None),
        P(),
        P(),
        P(None, "vocab"),
        P(None, "vocab"),
        P(),
        P("group"),
    )
    return jax.shard_map(
        local,
        mesh=mesh,
        in_specs=placed,
        out_specs=(P("group"), P(("group", "vocab"), None)),
        check_vma=False,
    )
```

```python
import functools

import jax
import jax.numpy as jnp
from jax import lax
from jax.experimental import pallas as pl
from jax.experimental.pallas import tpu as pltpu
from jax.sharding import PartitionSpec as P

MESH = pl.DeviceIdType.MESH
epsilon = 1e-06
loss_scale = 16.0
distill_mix = 0.5

RING = 4
CORES = 2
BLOCKS = RING * RING
SUB = 16
STEPS = (0, -1, 1, 2)
GATHER_COPIES = 6 + 6 * RING


def contract_last(left_side, right_side):
    return lax.dot_general(
        left_side, right_side, (((1,), (1,)), ((), ())), preferred_element_type=jnp.float32
    )


class Place:
    def __init__(self):
        self.group = lax.axis_index("group")
        self.vocab = lax.axis_index("vocab")
        self.core = lax.rem(self.vocab, CORES)
        self.zh = lax.rem(self.vocab // CORES, RING)
        self.x = self.vocab // (CORES * RING)

    def block(self, dx, dz):
        xx, zz = lax.rem(self.x + dx + RING, RING), lax.rem(self.zh + dz + RING, RING)
        return xx * RING + zz

    def dev(self, dx, dz):
        return (self.group, self.block(dx, dz) * CORES + self.core)

    def nth(self, d):
        return (self.group, lax.rem(self.block(0, 0) + d, BLOCKS) * CORES + self.core)

    def other(self):
        return (self.group, self.block(0, 0) * CORES + 1 - self.core)


class Gather:
    def __init__(self, buf, sem, place, sends):
        self.buf, self.sem, self.place, self.sends = buf, sem, place, sends
        self.width = buf.shape[2] // 2

    def copy(self, index, dx, dz, h, dev):
        view = self.buf.at[self.place.block(dx, dz), :, pl.ds(h * self.width, self.width)]
        return pltpu.make_async_remote_copy(
            src_ref=view,
            dst_ref=view,
            send_sem=self.sem.at[0, index],
            recv_sem=self.sem.at[1, index],
            device_id=dev,
            device_id_type=MESH,
        )

    def go(self, *args):
        copy = self.copy(*args)
        copy.start()
        self.sends.append(copy)

    def wait(self, index, dx, dz, h):
        self.copy(index, dx, dz, h, self.place.dev(1, 0)).wait_recv()

    def start(self):
        up, down = self.place.dev(0, 1), self.place.dev(0, -1)
        self.go(0, 0, 0, 0, up)
        self.go(2, 0, 0, 1, down)
        self.go(1, 0, 0, 1, up)
        self.go(3, 0, 0, 0, down)
        self.x_half(0, 0)
        self.x_half(0, 1)

    def x_half(self, j, h):
        up, down = self.place.dev(1, 0), self.place.dev(-1, 0)
        base, dz = 6 + 6 * j, STEPS[j]
        if h == 0:
            self.go(base, 0, dz, 0, up)
            self.go(base + 3, 0, dz, 0, down)
        else:
            self.go(base + 2, 0, dz, 1, down)
            self.go(base + 1, 0, dz, 1, up)

    def z_forward(self):
        self.wait(0, 0, -1, 0)
        self.go(4, 0, -1, 0, self.place.dev(0, 1))
        self.x_half(1, 0)
        self.wait(2, 0, 1, 1)
        self.go(5, 0, 1, 1, self.place.dev(0, -1))
        self.x_half(2, 1)

    def z_near(self):
        self.wait(1, 0, -1, 1)
        self.x_half(1, 1)
        self.wait(3, 0, 1, 0)
        self.x_half(2, 0)

    def z_far(self, direct):
        up, down, opposite = self.place.dev(1, 0), self.place.dev(-1, 0), self.place.dev(2, 0)
        base = 6 + 6 * 3
        self.wait(4, 0, 2, 0)
        if direct:
            self.go(base + 4, 0, 2, 0, opposite)
        self.go(base, 0, 2, 0, up)
        self.go(base + 3, 0, 2, 0, down)
        self.wait(5, 0, 2, 1)
        if direct:
            self.go(base + 5, 0, 2, 1, opposite)
        self.go(base + 2, 0, 2, 1, down)
        self.go(base + 1, 0, 2, 1, up)

    def x_forward(self, j):
        base, dz = 6 + 6 * j, STEPS[j]
        self.wait(base, -1, dz, 0)
        self.go(base + 4, -1, dz, 0, self.place.dev(1, 0))
        self.wait(base + 2, 1, dz, 1)
        self.go(base + 5, 1, dz, 1, self.place.dev(-1, 0))

    def x_last(self, h):
        base, dz = 6 + 6 * 3, STEPS[3]
        self.wait(base + h, -1, dz, h)
        self.wait(base + 3 - h, 1, dz, h)
        self.wait(base + 4 + h, 2, dz, h)

    def x_done(self, j, direct=False):
        base, dz = 6 + 6 * j, STEPS[j]
        if direct:
            self.wait(base, -1, dz, 0)
            self.wait(base + 2, 1, dz, 1)
        self.wait(base + 1, -1, dz, 1)
        self.wait(base + 3, 1, dz, 0)
        self.wait(base + 4, 2, dz, 0)
        self.wait(base + 5, 2, dz, 1)


def kernel(
    groups,
    teacher_rows_in,
    student_rows_in,
    teacher_gain_in,
    student_gain_in,
    teacher_head,
    student_head,
    route_in,
    target_in,
    loss_out,
    grad_out,
    teacher_rows,
    student_rows,
    teacher_gain,
    student_gain,
    route,
    target,
    head_t,
    head_s,
    rows_t,
    rows_s,
    wide,
    out_rows,
    in_rows,
    routed,
    hat_keep,
    inverse_keep,
    target_keep,
    logits_t,
    logits_s,
    exp_s,
    stat_all,
    columns_keep,
    part,
    xf_out,
    xf_in,
    xn_out,
    xn_in,
    z_part,
    zf_out,
    zf_in,
    zn_out,
    zn_in,
    local_sem,
    head_sem,
    route_sem,
    gather_t_sem,
    gather_s_sem,
    stat_sem,
    back_sem,
):
    p = Place()
    g, v, core = p.group, p.vocab, p.core
    f32, bf16 = jnp.float32, jnp.bfloat16
    local_rows, dt = teacher_rows.shape
    ds = student_rows.shape[1]
    shard = head_s.shape[2]
    ht, hs = dt // 2, ds // 2
    qs = hs // 2
    rows = BLOCKS * local_rows
    chunk = dt // SUB
    sends = []

    def remote(src, dst, sem, index, dev):
        copy = pltpu.make_async_remote_copy(
            src_ref=src,
            dst_ref=dst,
            send_sem=sem.at[0, index],
            recv_sem=sem.at[1, index],
            device_id=dev,
            device_id_type=MESH,
        )
        copy.start()
        sends.append(copy)
        return copy

    def fetch(src, dst, index):
        copy = pltpu.make_async_copy(src, dst, local_sem.at[index])
        copy.start()
        return copy

    barrier = pltpu.get_barrier_semaphore()

    def greet(dev):
        pl.semaphore_signal(barrier, inc=1, device_id=dev, device_id_type=MESH)

    load_rows_s = fetch(student_rows_in, student_rows, 0)
    load_gain_s = fetch(student_gain_in, student_gain, 1)
    load_rows_t = fetch(teacher_rows_in, teacher_rows, 2)
    load_gain_t = fetch(teacher_gain_in, teacher_gain, 3)
    load_route = fetch(route_in, route, 4)
    load_target = fetch(target_in, target, 5)
    load_head_s = fetch(student_head, head_s.at[core], 6)
    load_head_t = fetch(teacher_head, head_t.at[core], 7)
    for d in range(1, RING):
        greet(p.dev(d, 0))
    greet(p.dev(0, 1))
    greet(p.dev(0, -1))
    greet(p.other())
    for d in range(1, groups):
        greet((lax.rem(g + d, groups), v))

    load_rows_s.wait()
    load_gain_s.wait()
    here = p.block(0, 0)
    wide_s = student_rows[...].astype(f32)
    inverse = lax.rsqrt(jnp.mean(wide_s * wide_s, axis=1, keepdims=True) + epsilon)
    inverse_keep[...] = jnp.broadcast_to(inverse, inverse_keep.shape)
    hat = wide_s * inverse
    hat_keep[...] = hat
    gain_s = student_gain[...].astype(f32).reshape(1, ds)
    normed_s = hat * gain_s
    rows_s[here] = jnp.concatenate([normed_s[:, :hs], normed_s[:, hs:]], axis=0).astype(bf16)

    load_rows_t.wait()
    load_gain_t.wait()
    load_route.wait()
    wide_t = teacher_rows[...].astype(f32)
    inverse_t = lax.rsqrt(jnp.mean(wide_t * wide_t, axis=1, keepdims=True) + epsilon)
    normed_t = wide_t * inverse_t * teacher_gain[...].astype(f32).reshape(1, dt)
    for c in range(SUB):
        wide[:, c, :] = normed_t[:, c * chunk : (c + 1) * chunk]
    span = lax.axis_size("vocab") * local_rows
    first = g * span + v * local_rows
    my_routes = [route[first + k] for k in range(local_rows)]

    @pl.loop(0, groups)
    def _(dest):
        total = jnp.zeros((SUB, chunk), f32)
        for k in range(local_rows):
            total += jnp.where(my_routes[k] == dest, 1.0, 0.0) * wide[k]
        out_rows[dest] = total.astype(bf16)

    in_rows[g] = out_rows[g]
    pl.semaphore_wait(barrier, groups - 1 + RING - 1 + 2 + 1)

    student = Gather(rows_s, gather_s_sem, p, sends)
    teacher = Gather(rows_t, gather_t_sem, p, sends)
    student.start()

    routed_copies = []
    for d in range(1, groups):
        dest = lax.rem(g + d, groups)
        routed_copies.append(
            remote(out_rows.at[dest], in_rows.at[g], route_sem, d, (dest, v))
        )
    fetch_head_s = remote(student_head, head_s.at[core], head_sem, 0, p.other())
    fetch_head_t = remote(teacher_head, head_t.at[core], head_sem, 1, p.other())

    student.x_forward(0)
    student.z_forward()
    student.z_near()

    ranks, valids = [], []
    seen = jnp.int32(0)
    for t in range(groups):
        start = t * span + v * local_rows
        valid = jnp.int32(0)
        for k in range(local_rows):
            valid += jnp.where(route[start + k] == g, 1, 0)
        ranks.append(seen)
        valids.append(valid)
        seen = seen + valid
    for copy in routed_copies:
        copy.wait_recv()
    for j in range(local_rows):
        total = jnp.zeros((SUB, chunk), f32)
        for t in range(groups):
            weight = jnp.where(ranks[t] == j, valids[t], 0).astype(f32)
            total += weight * in_rows[t].astype(f32)
        wide[j] = total
    for c in range(SUB):
        half, at = divmod(c * chunk, ht)
        routed[half * 8 : half * 8 + 8, at : at + chunk] = wide[:, c, :]
    rows_t[here] = routed[...].astype(bf16)
    teacher.start()

    teacher.x_forward(0)
    student.z_far(False)
    student.x_forward(1)
    student.x_forward(2)
    teacher.z_forward()
    teacher.z_near()
    student.x_forward(3)

    load_target.wait()
    all_targets = jnp.transpose(jnp.broadcast_to(target[...].astype(f32), (128, 2 * rows)))
    target_keep[...] = all_targets
    columns = (v // CORES) * (CORES * shard) + lax.broadcasted_iota(
        jnp.int32, (rows, CORES * shard), 1
    )
    my_targets = jnp.concatenate(
        [
            target_keep[pl.ds(pl.multiple_of(b * 16 + core * 8, 8), 8), :]
            for b in range(BLOCKS)
        ],
        axis=0,
    )[:, 0:1].astype(jnp.int32)

    def logits(left, count, head, half):
        parts = []
        for c in range(CORES):
            low = jnp.dot(left, head[c, 0:half, :], preferred_element_type=f32)
            high = jnp.dot(left, head[c, half : 2 * half, :], preferred_element_type=f32)
            low = low.reshape(count, 16, shard)[:, 0:8]
            high = high.reshape(count, 16, shard)[:, 8:16]
            parts.append((low + high).reshape(count * 8, shard))
        return jnp.concatenate(parts, axis=1)

    teacher.x_forward(1)
    teacher.x_forward(2)
    teacher.z_far(True)
    for j in range(RING):
        student.x_done(j)
    load_head_s.wait()
    fetch_head_s.wait_recv()
    values = logits(rows_s[...].reshape(BLOCKS * 16, hs), BLOCKS, head_s, hs)
    logits_s[...] = values
    top_s = jnp.max(values, axis=1, keepdims=True)
    powers = jnp.exp(values - top_s)
    exp_s[...] = powers
    sum_s = jnp.sum(powers, axis=1, keepdims=True)
    picked = jnp.sum(jnp.where(columns == my_targets, values, 0.0), axis=1, keepdims=True)


    def teacher_logits(steps):
        blocks = [p.block(dx, STEPS[j]) for j in steps for dx in range(RING)]
        left = jnp.concatenate([rows_t[b] for b in blocks], axis=0)
        values = logits(left, len(blocks), head_t, ht)
        for i, b in enumerate(blocks):
            logits_t[pl.ds(pl.multiple_of(b * 8, 8), 8), :] = values[i * 8 : i * 8 + 8]

    load_head_t.wait()
    fetch_head_t.wait_recv()
    for j in range(3):
        teacher.x_done(j)
    teacher_logits((0, 1, 2))
    blocks = [p.block(dx, STEPS[3]) for dx in range(RING)]
    sums = [0.0] * CORES
    for h in range(2):
        teacher.x_last(h)
        near, far = h * (ht // 2), ht + h * (ht // 2)
        left = jnp.concatenate([rows_t[b, :, near : near + ht // 2] for b in blocks], axis=0)
        for c in range(CORES):
            low = jnp.dot(left, head_t[c, near : near + ht // 2, :], preferred_element_type=f32)
            high = jnp.dot(left, head_t[c, far : far + ht // 2, :], preferred_element_type=f32)
            low, high = (value.reshape(RING, 16, shard) for value in (low, high))
            sums[c] = sums[c] + (low[:, 0:8] + high[:, 8:16]).reshape(RING * 8, shard)
    values = jnp.concatenate(sums, axis=1)
    for i, b in enumerate(blocks):
        logits_t[pl.ds(pl.multiple_of(b * 8, 8), 8), :] = values[i * 8 : i * 8 + 8]

    values = logits_t[...]
    top_t = jnp.max(values, axis=1, keepdims=True)
    exp_t = jnp.exp(values - top_t)
    sum_t = jnp.sum(exp_t, axis=1, keepdims=True)
    cross = jnp.sum(exp_t * (values - logits_s[...]), axis=1, keepdims=True)

    lane = lax.broadcasted_iota(jnp.int32, (rows, 128), 1)
    packed = jnp.zeros((rows, 128), f32)
    for i, value in enumerate((top_t, top_s, top_t, None, sum_t, sum_s, cross, picked)):
        if value is not None:
            packed = jnp.where(lane == i, value, packed)
    stats = jnp.transpose(packed)[0:8, :]

    stat_all[here] = stats
    copies = [
        remote(stat_all.at[here], stat_all.at[here], stat_sem, d, p.nth(d))
        for d in range(1, BLOCKS)
    ]
    for copy in copies:
        copy.wait_recv()
    parts = [stat_all[i] for i in range(BLOCKS)]
    tops = functools.reduce(jnp.maximum, [part[0:4] for part in parts])
    sums = sum(jnp.exp(part[0:4] - tops) * part[4:8] for part in parts)
    merged = jnp.concatenate([tops, sums], axis=0)
    all_top_t, all_top_s = merged[0:1], merged[1:2]
    all_sum_t, all_sum_s = merged[4:5], merged[5:6]
    scale_t = (loss_scale * distill_mix) * jnp.exp(stats[0:1] - all_top_t) / all_sum_t
    scale_s = loss_scale * jnp.exp(stats[1:2] - all_top_s) / all_sum_s
    lse_t = all_top_t + jnp.log(all_sum_t)
    lse_s = all_top_s + jnp.log(all_sum_s)
    loss = distill_mix * (merged[6:7] / all_sum_t - lse_t + lse_s) + (1.0 - distill_mix) * (
        lse_s - merged[7:8]
    )
    turned = jnp.transpose(
        jnp.concatenate([scale_t, scale_s, loss, jnp.zeros((125, rows), f32)], axis=0)
    )
    columns_keep[core] = turned
    loss_copy = remote(columns_keep.at[core], columns_keep.at[core], head_sem, 2, p.other())
    logit_grad = (
        exp_s[...] * turned[:, 1:2]
        - exp_t * turned[:, 0:1]
        - jnp.where(columns == my_targets, loss_scale * (1.0 - distill_mix), 0.0)
    ).astype(bf16)

    order = (2, 1, -1, 0)
    plus_x, minus_x = p.dev(1, 0), p.dev(-1, 0)
    plus_z, minus_z = p.dev(0, 1), p.dev(0, -1)
    cols = (slice(0, qs), slice(qs, hs))
    far_copies, near_copies = {}, {}

    def x_first(i):
        far, up, down = (part.at[p.block(d, order[i])] for d in (2, 1, -1))
        xf_out[i, 0] = far[:, cols[0]].astype(bf16)
        xf_out[i, 1] = far[:, cols[1]].astype(bf16)
        far_copies[i] = (
            remote(xf_out.at[i, 0], xf_in.at[i, 0], back_sem, 2 * i, plus_x),
            remote(xf_out.at[i, 1], xf_in.at[i, 1], back_sem, 1 + 2 * i, minus_x),
        )
        xn_out[i, 0, 1] = up[:, cols[1]].astype(bf16)
        xn_out[i, 1, 0] = down[:, cols[0]].astype(bf16)
        near_copies[i] = [
            remote(xn_out.at[i, 0, 1], xn_in.at[i, 0, 1], back_sem, 8 + 2 * i, plus_x),
            remote(xn_out.at[i, 1, 0], xn_in.at[i, 1, 0], back_sem, 9 + 2 * i, minus_x),
        ]

    def x_whole(i, h):
        slots = (xf_out.at[i, h], xn_out.at[i, 0, h], xn_out.at[i, 1, h])
        for slot, d in zip(slots, (2, 1, -1)):
            slot[...] = part[p.block(d, order[i]), :, cols[h]].astype(bf16)
        return (
            remote(slots[0], xf_in.at[i, h], back_sem, 2 * i + h, p.dev(2, 0)),
            remote(slots[1], xn_in.at[i, 0, h], back_sem, 16 - 8 * h + 2 * i, plus_x),
            remote(slots[2], xn_in.at[i, 1, h], back_sem, 9 + 8 * h + 2 * i, minus_x),
        )

    def x_second(i):
        up, down = (part.at[p.block(d, order[i])] for d in (1, -1))
        far_copies[i][0].wait_recv()
        xn_out[i, 0, 0] = (up[:, cols[0]] + xf_in[i, 0].astype(f32)).astype(bf16)
        near_copies[i].append(
            remote(xn_out.at[i, 0, 0], xn_in.at[i, 0, 0], back_sem, 16 + 2 * i, plus_x)
        )
        far_copies[i][1].wait_recv()
        xn_out[i, 1, 1] = (down[:, cols[1]] + xf_in[i, 1].astype(f32)).astype(bf16)
        near_copies[i].append(
            remote(xn_out.at[i, 1, 1], xn_in.at[i, 1, 1], back_sem, 17 + 2 * i, minus_x)
        )

    def x_done(i):
        for copy in near_copies[i]:
            copy.wait_recv()
        block = part.at[p.block(0, order[i])]
        return [
            block[:, cols[h]] + xn_in[i, 0, h].astype(f32) + xn_in[i, 1, h].astype(f32)
            for h in range(2)
        ]

    step = qs // 2
    whole_copies = []
    for h in range(2):
        for n in (2 * h, 2 * h + 1, 2 * h + 4, 2 * h + 5):
            half, at = divmod(n * step, hs)
            block = contract_last(
                logit_grad[:, 0:shard], head_s[0, n * step : (n + 1) * step, :]
            ) + contract_last(logit_grad[:, shard:], head_s[1, n * step : (n + 1) * step, :])
            part[:, half * 8 : half * 8 + 8, at : at + step] = block.reshape(
                BLOCKS, local_rows, step
            )
        whole_copies.append(x_whole(0, h))
    x_first(1)
    x_first(2)
    x_first(3)
    x_second(1)
    x_second(2)
    z_far = []
    for h in range(2):
        for copy in whole_copies[h]:
            copy.wait_recv()
        zf_out[h] = (
            part[p.block(0, order[0]), :, cols[h]]
            + xf_in[0, h].astype(f32)
            + xn_in[0, 0, h].astype(f32)
            + xn_in[0, 1, h].astype(f32)
        ).astype(bf16)
        z_far.append(
            remote(zf_out.at[h], zf_in.at[h], back_sem, 24 + h, (plus_z, minus_z)[h])
        )
    x_second(3)
    up = x_done(1)
    zn_out[0, 1] = up[1].astype(bf16)
    z_near = [remote(zn_out.at[0, 1], zn_in.at[0, 1], back_sem, 26, plus_z)]
    z_part[0] = up[0]
    down = x_done(2)
    zn_out[1, 0] = down[0].astype(bf16)
    z_near.append(remote(zn_out.at[1, 0], zn_in.at[1, 0], back_sem, 27, minus_z))
    z_part[1] = down[1]
    z_far[0].wait_recv()
    zn_out[0, 0] = (z_part[0] + zf_in[0].astype(f32)).astype(bf16)
    z_near.append(remote(zn_out.at[0, 0], zn_in.at[0, 0], back_sem, 28, plus_z))
    z_far[1].wait_recv()
    zn_out[1, 1] = (z_part[1] + zf_in[1].astype(f32)).astype(bf16)
    z_near.append(remote(zn_out.at[1, 1], zn_in.at[1, 1], back_sem, 29, minus_z))
    for h, value in enumerate(x_done(3)):
        z_part[2 + h] = value

    loss_copy.wait_recv()
    both = jnp.concatenate(
        [columns_keep[c, b * 8 : b * 8 + 8, :] for b in range(BLOCKS) for c in range(CORES)],
        axis=0,
    )
    loss_out[...] = jnp.transpose(both)[2:3, :]
    inverse = inverse_keep[:, 0:1]
    hat = hat_keep[...]
    gain = student_gain[...].astype(f32).reshape(1, ds)

    for copy in z_near:
        copy.wait_recv()
    mine = [
        z_part[2 + h] + zn_in[0, h].astype(f32) + zn_in[1, h].astype(f32) for h in range(2)
    ]
    scaled = (
        jnp.concatenate([mine[0][0:8], mine[1][0:8], mine[0][8:16], mine[1][8:16]], axis=1)
        * gain
    )
    grad_out[...] = (
        inverse * (scaled - hat * jnp.mean(scaled * hat, axis=1, keepdims=True))
    ).astype(bf16)

    for copy in sends:
        copy.wait_send()


def local(
    teacher_rows,
    student_rows,
    teacher_gain,
    student_gain,
    teacher_head,
    student_head,
    route,
    target,
):
    groups = lax.axis_size("group")
    f32, bf16 = jnp.float32, jnp.bfloat16
    local_rows, dt = teacher_rows.shape
    ds = student_rows.shape[1]
    shard = teacher_head.shape[1]
    all_rows = target.shape[0]
    rows = all_rows // CORES
    ht, hs = dt // 2, ds // 2
    qs, chunk = hs // 2, dt // SUB
    vmem = pl.BlockSpec(memory_space=pltpu.VMEM)
    anywhere = pl.BlockSpec(memory_space=pl.ANY)
    loss, grad = pl.pallas_call(
        functools.partial(kernel, groups),
        out_shape=(
            jax.ShapeDtypeStruct((1, all_rows), f32),
            jax.ShapeDtypeStruct((local_rows, ds), bf16),
        ),
        in_specs=[anywhere] * 8,
        out_specs=(vmem, vmem),
        scratch_shapes=[
            pltpu.VMEM((local_rows, dt), bf16),
            pltpu.VMEM((local_rows, ds), bf16),
            pltpu.VMEM((dt,), bf16),
            pltpu.VMEM((ds,), bf16),
            pltpu.SMEM(route.shape, jnp.int32),
            pltpu.VMEM((1, all_rows), jnp.int32),
            pltpu.VMEM((CORES, dt, shard), bf16),
            pltpu.VMEM((CORES, ds, shard), bf16),
            pltpu.VMEM((BLOCKS, 16, ht), bf16),
            pltpu.VMEM((BLOCKS, 16, hs), bf16),
            pltpu.VMEM((local_rows, SUB, chunk), f32),
            pltpu.VMEM((groups, SUB, chunk), bf16),
            pltpu.VMEM((groups, SUB, chunk), bf16),
            pltpu.VMEM((16, ht), f32),
            pltpu.VMEM((local_rows, ds), f32),
            pltpu.VMEM((local_rows, 128), f32),
            pltpu.VMEM((all_rows, 128), f32),
            pltpu.VMEM((rows, CORES * shard), f32),
            pltpu.VMEM((rows, CORES * shard), f32),
            pltpu.VMEM((rows, CORES * shard), f32),
            pltpu.VMEM((BLOCKS, 8, rows), f32),
            pltpu.VMEM((CORES, rows, 128), f32),
            pltpu.VMEM((BLOCKS, 16, hs), f32),
            pltpu.VMEM((4, 2, 16, qs), bf16),
            pltpu.VMEM((4, 2, 16, qs), bf16),
            pltpu.VMEM((4, 2, 2, 16, qs), bf16),
            pltpu.VMEM((4, 2, 2, 16, qs), bf16),
            pltpu.VMEM((4, 16, qs), f32),
            pltpu.VMEM((2, 16, qs), bf16),
            pltpu.VMEM((2, 16, qs), bf16),
            pltpu.VMEM((2, 2, 16, qs), bf16),
            pltpu.VMEM((2, 2, 16, qs), bf16),
            pltpu.SemaphoreType.DMA((8,)),
            pltpu.SemaphoreType.DMA((2, 3)),
            pltpu.SemaphoreType.DMA((2, groups)),
            pltpu.SemaphoreType.DMA((2, GATHER_COPIES)),
            pltpu.SemaphoreType.DMA((2, GATHER_COPIES)),
            pltpu.SemaphoreType.DMA((2, BLOCKS)),
            pltpu.SemaphoreType.DMA((2, 30)),
        ],
        compiler_params=pltpu.CompilerParams(
            collective_id=0, has_side_effects=True, vmem_limit_bytes=60 * 1024 * 1024
        ),
        name="distill",
    )(
        teacher_rows,
        student_rows,
        teacher_gain,
        student_gain,
        teacher_head,
        student_head,
        route,
        target.reshape(1, all_rows),
    )
    return (loss.reshape(all_rows), grad)


def solution(mesh):
    placed = (
        P(("group", "vocab"), None),
        P(("group", "vocab"), None),
        P(),
        P(),
        P(None, "vocab"),
        P(None, "vocab"),
        P(),
        P("group"),
    )
    return jax.shard_map(
        local,
        mesh=mesh,
        in_specs=placed,
        out_specs=(P("group"), P(("group", "vocab"), None)),
        check_vma=False,
    )
```
